32 devices in a mesh: groups: 2 (over y), gz: 4 (over x, core), xy: 4 (over z).
Axes of the slice: x: 2, y: 2, z: 4, core: 2. Of those that a mesh axis runs over, the one named last changes fastest.
Arguments:
- features: bfloat16 [16, 32, 32, 128], P(('groups', 'gz'), 'xy'), parts along dimension 0, may hold values from -6 to 6
- species: int32 [16, 32, 32], P(('groups', 'gz'), 'xy'), parts along dimension 0, may hold values from 0 to 7
- sublayer: int32 [16, 32, 32], P(('groups', 'gz'), 'xy'), parts along dimension 0, may hold values from 0 to 1
- offsets: float32 [2, 16, 32, 32], P(None, ('groups', 'gz'), 'xy'), parts along dimension 1, may hold values from 0 to 11
- neighbours: int32 [16, 32, 32, 32], P(('groups', 'gz'), 'xy'), parts along dimension 0, may hold values from 0 to 287
- neighbour_count: int32 [16, 32, 32], P(('groups', 'gz'), 'xy'), parts along dimension 0, may hold values from 16 to 32
- distances: float32 [16, 32, 32, 32], P(('groups', 'gz'), 'xy'), parts along dimension 0, may hold values from 0.8 to 7.8
- species_table: bfloat16 [8, 128], replicated, may hold values from -3 to 3
- charge_weight: bfloat16 [128, 16], replicated, may hold values from -0.5 to 0.5
- radial_in: bfloat16 [8, 64], replicated, may hold values from -2 to 2
- radial_out: bfloat16 [64, 128], replicated, may hold values from -0.75 to 0.75
- update_in: bfloat16 [128, 256], replicated, may hold values from -0.5 to 0.5
- update_out: bfloat16 [256, 128], replicated, may hold values from -0.375 to 0.375
- energy_weight: bfloat16 [128], replicated, may hold values from -0.5 to 0.5
Outputs:
- features_out: bfloat16 [16, 32, 32, 128], P(('groups', 'gz'), 'xy'), parts along dimension 0
- energy: float32 [16, 32, 32], P(('groups', 'gz'), 'xy'), parts along dimension 0
- forces: float32 [2, 16, 32, 32], P(None, ('groups', 'gz'), 'xy'), parts along dimension 1
The draws below stay inside these ranges and needn't reach their ends.
There are 2 independent parts, one for each index of `groups`. The reference program is written for one: setup_inputs(seed, part) draws one part's arguments, and reference() takes and returns one part's arrays. A program takes and returns all parts, laid end to end along the dimension named above; an argument that names none is the same for every part. Nothing has to cross between parts.
Inputs may be any that keep to these rules, and one draw needn't show every extreme that they name: `neighbours`: an entry n names the neighbour at cell offset o = n // 32 (z offset o // 3 - 1, x offset o % 3 - 1) and slot n % 32 of that cell. `neighbour_count`: entries of a list from this count on are padding.
All inputs are finite; a program needn't handle non-finite values.
Results may differ from the reference program's by a relative error of at most 0.0012.
The reference program's roundings to bfloat16 on the way count: a program that leaves them out, or rounds other values in their place, can miss the bound.
Values may be sent and summed in bfloat16 or wider, within the bound.
A program may use at most 64 MiB of HBM per device.

```python
import math
import jax
import jax.numpy as jnp
from jax import lax

F = 128
C = 16
KX = 128
KY = 8
RH = 64
FH = 256
NRBF = 8
NSPEC = 8
NB = 32
SLOT = 32
NZ = 8
NX = 32


def with_ends(drawn, stream_key, least, largest):
    place = [jax.random.randint(jax.random.fold_in(stream_key, axis), (), 0, length) for axis, length in enumerate(drawn.shape)]
    main_axis = drawn.shape.index(max(drawn.shape))
    next_to = place[:main_axis] + [(place[main_axis] + 1) % drawn.shape[main_axis]] + place[main_axis + 1:]
    return drawn.at[tuple(place)].set(least).at[tuple(next_to)].set(largest)


def steps_of(rng, dims, shards, smallest, top_value):
    def one(dim, blocks):
        steps = jax.random.uniform(jax.random.fold_in(jax.random.fold_in(rng, 6), dim), (blocks,), jnp.float32, smallest / len(shards), top_value / len(shards))
        return jnp.repeat(jnp.exp(steps), dims[dim] // blocks).reshape((-1,) + (1,) * (len(dims) - dim - 1))

    level = one(*shards[0])
    for cut in shards[1:]:
        level = level * one(*cut)
    return level


def gaussian(key, shape, scale, most, split=(), kind=jnp.bfloat16):
    entries = jax.random.normal(key, shape, jnp.float32) * scale
    if len(split) > 0:
        entries = steps_of(key, shape, split, -0.22, 0.18) * entries
    return jnp.clip(entries, min=-most, max=most).astype(kind)


def setup_inputs(seed: int = 0, part: int = 0) -> dict:
    seeds = jax.random.split(jax.random.key(seed), 15)
    part_keys = jax.random.split(jax.random.fold_in(seeds[14], part), 15)
    features = gaussian(part_keys[0], (NZ, NX, SLOT, F), 1.0, 6.0, ((0, 4), (1, 4)))
    species = with_ends(jax.random.randint(part_keys[1], (NZ, NX, SLOT), 0, NSPEC), jax.random.fold_in(part_keys[1], 1), 0, NSPEC - 1).astype(jnp.int32)
    sublayer = with_ends(jax.random.randint(part_keys[2], (NZ, NX, SLOT), 0, 2), jax.random.fold_in(part_keys[2], 1), 0, 1).astype(jnp.int32)
    offsets = jnp.clip(11.0 * jax.random.uniform(part_keys[3], (2, NZ, NX, SLOT), jnp.float32) ** steps_of(part_keys[3], (2, NZ, NX, SLOT), ((1, 4), (2, 4)), -0.2, 0.2), 0.0, 11.0)
    neighbours = with_ends(jax.random.randint(part_keys[4], (NZ, NX, SLOT, NB), 0, 9 * SLOT), jax.random.fold_in(part_keys[4], 1), 0, (9 * SLOT) - 1).astype(jnp.int32)
    neighbour_count = with_ends(jax.random.randint(part_keys[5], (NZ, NX, SLOT), NB // 2, NB + 1), jax.random.fold_in(part_keys[5], 1), NB // 2, NB).astype(jnp.int32)
    distances = jnp.clip(0.8 + 7 * jax.random.uniform(part_keys[6], (NZ, NX, SLOT, NB), jnp.float32) ** steps_of(part_keys[6], (NZ, NX, SLOT, NB), ((0, 4), (1, 4)), -0.2, 0.2), 0.8, 7.8)
    species_table = gaussian(seeds[7], (NSPEC, F), 0.5, 3.0)
    charge_weight = gaussian(seeds[8], (F, C), F ** -0.5, 0.5)
    radial_in = gaussian(seeds[9], (NRBF, RH), NRBF ** -0.5, 2.0)
    radial_out = gaussian(seeds[10], (RH, F), RH ** -0.5, 0.75)
    update_in = gaussian(seeds[11], (F, FH), F ** -0.5, 0.5)
    update_out = gaussian(seeds[12], (FH, F), FH ** -0.5, 0.375)
    energy_weight = gaussian(seeds[13], (F,), F ** -0.5, 0.5)
    return dict(features=features, species=species, sublayer=sublayer, offsets=offsets, neighbours=neighbours, neighbour_count=neighbour_count, distances=distances, species_table=species_table, charge_weight=charge_weight, radial_in=radial_in, radial_out=radial_out, update_in=update_in, update_out=update_out, energy_weight=energy_weight)


cell_width = 11.0
layer_depth = 5.5
screening = 0.025
smearing = 1.0
coupling = 0.25
cutoff = 8.0
basis_width = 1.0

def wave_numbers(wave_index, width_x):
    wave_x = 2.0 * math.pi / width_x * (wave_index // KY - KX // 2).astype(jnp.float32)
    wave_y = 2.0 * math.pi / cell_width * (wave_index % KY - KY // 2).astype(jnp.float32)
    return (wave_x, wave_y)

def wave_factors(wave_x, wave_y, width_x):
    square = wave_x * wave_x + wave_y * wave_y
    screened = jnp.sqrt(square + screening * screening)
    weight = coupling * (2.0 * math.pi / (width_x * cell_width)) * jnp.exp(-0.5 * smearing * smearing * square) / screened
    return (screened, weight)

def build_panel(layer_field, wave_x, wave_y, weight):
    cosine = layer_field[:, :, 0] * weight
    sin_part = layer_field[:, :, 1] * weight
    cos_rows = jnp.stack([cosine, wave_x * sin_part, wave_y * sin_part], axis=1)
    sin_rows = jnp.stack([sin_part, -wave_x * cosine, -wave_y * cosine], axis=1)
    field_panel = jnp.stack([cos_rows, sin_rows], axis=3)
    shape = field_panel.shape
    return field_panel.reshape(shape[0], 3 * shape[2], 2, shape[4]).astype(jnp.bfloat16)

def phase_table(coord_x, coord_y, wave_x, wave_y):
    angles = coord_x[..., None] * wave_x + coord_y[..., None] * wave_y
    return jnp.concatenate([jnp.cos(angles), jnp.sin(angles)], axis=-1).astype(jnp.bfloat16)

def reference(features, species, sublayer, offsets, neighbours, neighbour_count, distances, species_table, charge_weight, radial_in, radial_out, update_in, update_out, energy_weight):
    z_count, x_count, slot_count, feature_width = features.shape
    channels = charge_weight.shape[1]
    wave_count = KX * KY
    width_x = cell_width * x_count
    hidden_start = (features.astype(jnp.float32) + species_table[species].astype(jnp.float32)).astype(jnp.bfloat16)
    charges = jnp.dot(hidden_start.reshape(-1, feature_width), charge_weight, preferred_element_type=jnp.float32)
    charges = charges.astype(jnp.bfloat16).reshape(z_count, x_count, slot_count, channels)
    wave_x, wave_y = wave_numbers(jnp.arange(wave_count, dtype=jnp.int32), width_x)
    screened, weight = wave_factors(wave_x, wave_y, width_x)
    decay = jnp.exp(-screened * layer_depth)
    cell_x = jnp.arange(x_count, dtype=jnp.int32).astype(jnp.float32)
    coord_x = cell_width * cell_x[None, :, None] + offsets[0]
    coord_y = offsets[1]

    def row_phases(z_row):
        return phase_table(coord_x[z_row].reshape(-1), coord_y[z_row].reshape(-1), wave_x, wave_y)

    def row_moments(z_row):
        phases = row_phases(z_row)
        layer_mask = (sublayer[z_row][..., None] == jnp.arange(2, dtype=jnp.int32)).astype(jnp.bfloat16)
        weighted = (layer_mask[..., :, None] * charges[z_row][..., None, :]).reshape(-1, 2 * channels)
        return jnp.dot(weighted.T, phases, preferred_element_type=jnp.float32)
    raw_moments = lax.map(row_moments, jnp.arange(z_count, dtype=jnp.int32))
    moments = raw_moments.reshape(2 * z_count, channels, 2, wave_count)

    def down_step(carried, layer_moments):
        renewed_sum = decay * carried + layer_moments
        return (renewed_sum, renewed_sum)

    def up_step(carried, layer_moments):
        return (decay * (carried + layer_moments), carried)
    start_carry = jnp.zeros((channels, 2, wave_count), jnp.float32)
    _, from_below = lax.scan(down_step, start_carry, moments)
    _, from_above = lax.scan(up_step, start_carry, moments, reverse=True)
    layer_field = from_below + from_above
    field_panel = build_panel(layer_field, wave_x, wave_y, weight).reshape(2 * z_count, 3 * channels, 2 * wave_count)
    z_padded = jnp.pad(hidden_start, ((1, 1), (0, 0), (0, 0), (0, 0)))
    padded = jnp.concatenate([z_padded[:, -1:], z_padded, z_padded[:, :1]], axis=1)
    own_slot = jnp.arange(slot_count, dtype=jnp.int32)[None, :, None]
    listed = jnp.arange(neighbours.shape[3], dtype=jnp.int32)
    cell_range = jnp.arange(x_count, dtype=jnp.int32)[:, None, None]
    basis_count = radial_in.shape[0]
    centers = cutoff * jnp.arange(basis_count, dtype=jnp.int32).astype(jnp.float32) / (basis_count - 1)

    def row_outputs(z_row):
        phases = row_phases(z_row)
        panel_pair = lax.dynamic_slice_in_dim(field_panel, 2 * z_row, 2, 0).reshape(6 * channels, 2 * wave_count)
        evaluated = lax.dot_general(phases, panel_pair, (((1,), (1,)), ((), ())), preferred_element_type=jnp.float32)
        evaluated = evaluated.reshape(x_count, slot_count, 2, 3, channels)
        chosen = jnp.where((sublayer[z_row] == 0)[..., None, None], evaluated[:, :, 0], evaluated[:, :, 1])
        charge_values = charges[z_row].astype(jnp.float32)
        long_energy = 0.5 * lax.optimization_barrier(jnp.sum(charge_values * chosen[:, :, 0], axis=-1))
        force_x = -lax.optimization_barrier(jnp.sum(charge_values * chosen[:, :, 1], axis=-1))
        force_y = -lax.optimization_barrier(jnp.sum(charge_values * chosen[:, :, 2], axis=-1))
        region = lax.dynamic_slice_in_dim(padded, z_row, 3, 0).reshape(-1, feature_width)
        codes = neighbours[z_row]
        offset_code = codes // slot_count
        slot_code = codes % slot_count
        row_index = (offset_code // 3 * (x_count + 2) + cell_range + offset_code % 3) * slot_count + slot_code
        gathered = jnp.take(region, row_index.reshape(-1), axis=0).reshape(x_count, slot_count, -1, feature_width)
        usable = (listed < neighbour_count[z_row][..., None]) & jnp.logical_not((offset_code == 4) & (slot_code == own_slot))
        spacing = distances[z_row]
        radial_basis = jnp.exp(-jnp.square((spacing[..., None] - centers) / basis_width)).astype(jnp.bfloat16)
        filter_hidden = jax.nn.silu(jnp.dot(radial_basis.reshape(-1, basis_count), radial_in, preferred_element_type=jnp.float32)).astype(jnp.bfloat16)
        filters = jnp.dot(filter_hidden, radial_out, preferred_element_type=jnp.float32).reshape(gathered.shape)
        envelope = jnp.square(1.0 - jnp.square(spacing / cutoff))
        edge_weight = jnp.where(usable, envelope, 0.0)
        aggregate = lax.optimization_barrier(jnp.sum(edge_weight[..., None] * filters * gathered.astype(jnp.float32), axis=2)).astype(jnp.bfloat16)
        update_hidden = jax.nn.silu(jnp.dot(aggregate.reshape(-1, feature_width), update_in, preferred_element_type=jnp.float32)).astype(jnp.bfloat16)
        renewed = hidden_start[z_row].astype(jnp.float32) + jnp.dot(update_hidden, update_out, preferred_element_type=jnp.float32).reshape(x_count, slot_count, feature_width)
        energy_row = lax.optimization_barrier(jnp.sum(renewed * energy_weight.astype(jnp.float32), axis=-1)) + long_energy
        return (renewed.astype(jnp.bfloat16), energy_row, jnp.stack([force_x, force_y]))
    features_out, energy, force_rows = lax.map(row_outputs, jnp.arange(z_count, dtype=jnp.int32))
    forces = jnp.moveaxis(force_rows, 1, 0)
    return (features_out, energy, forces)
```

```python
import functools
import math

import jax
import jax.numpy as jnp
import numpy as np
from jax import lax
from jax.experimental import pallas as pl
from jax.experimental.pallas import tpu as pltpu
from jax.sharding import PartitionSpec as P

KX = 128
KY = 8
MESH = pl.DeviceIdType.MESH

cell_width = 11.0
layer_depth = 5.5
screening = 0.025
smearing = 1.0
coupling = 0.25
cutoff = 8.0

BLOCKS = (4, 0, 5, 6, 7)
WAVES = KX * len(BLOCKS)


def wave_constants(width_x, layers):
    index_x = np.tile(np.arange(KX), len(BLOCKS))
    index_y = np.repeat(np.array(BLOCKS), KX)
    count = np.ones(WAVES, np.float32)
    count[2 * KX :][index_x[2 * KX :] > 0] = 2.0
    count[1 : KX // 2] = 2.0
    count[KX // 2 + 1 : KX] = 0.0
    for spare, j in enumerate((1, 2, 3)):
        index_x[KX // 2 + 1 + spare] = 0
        index_y[KX // 2 + 1 + spare] = j
        count[KX // 2 + 1 + spare] = 1.0
    f32 = np.float32
    wave_x = f32(2.0 * math.pi / width_x) * (index_x - KX // 2).astype(f32)
    wave_y = f32(2.0 * math.pi / cell_width) * (index_y - KY // 2).astype(f32)
    square = wave_x * wave_x + wave_y * wave_y
    screened = np.sqrt(square + f32(screening * screening))
    weight = f32(coupling * (2.0 * math.pi / (width_x * cell_width))) * np.exp(
        f32(-0.5 * smearing * smearing) * square
    )
    weight = weight / screened * count
    row_x = np.zeros(WAVES, f32)
    row_x[:KX] = f32(2.0 * math.pi / width_x) * (np.arange(KX) - KX // 2).astype(f32)
    row_y = np.zeros(WAVES, f32)
    row_y[: len(BLOCKS) - 1] = f32(2.0 * math.pi / cell_width) * (
        np.array(BLOCKS[1:]) - KY // 2
    ).astype(f32)
    powers = [np.exp(-screened * f32(layer_depth) * f32(n)) for n in range(layers + 1)]
    rows = [wave_x, wave_y, weight, row_x, row_y] + powers
    rows += [np.zeros(WAVES, f32)] * (-len(rows) % 8)
    return np.stack(rows).astype(f32)


def sincos(angle):
    turns = jnp.floor(angle * (2.0 / math.pi) + 0.5)
    rest = angle - turns * 1.5703125
    rest = rest - turns * 4.8375129699707031e-4
    rest = rest - turns * 7.5497899548918822e-8
    square = rest * rest
    sine = rest + rest * square * (
        (-1.9515295891e-4 * square + 8.3321608736e-3) * square - 1.6666654611e-1
    )
    cosine = (1.0 - 0.5 * square) + square * square * (
        (2.443315711809948e-5 * square - 1.388731625493765e-3) * square + 4.166664568298827e-2
    )
    quadrant = turns.astype(jnp.int32)
    swap = (quadrant & 1) == 1
    out_sin = jnp.where(swap, cosine, sine)
    out_cos = jnp.where(swap, sine, cosine)
    out_sin = jnp.where((quadrant & 2) == 2, -out_sin, out_sin)
    out_cos = jnp.where(((quadrant + 1) & 2) == 2, -out_cos, out_cos)
    return out_sin, out_cos


def silu(value):
    half = 0.5 * value
    return half + half * jnp.tanh(half)


def dot(a, b):
    return jnp.dot(a, b, preferred_element_type=jnp.float32)


def kernel(
    sizes,
    feat,
    atom_rows,
    near,
    dist,
    table,
    charge_cols,
    hidden_in,
    hidden_out,
    update_in,
    update_out,
    energy_w,
    cst,
    spread,
    centers,
    out_feat,
    out_rows,
    ext,
    ph,
    fh,
    wgt,
    agg,
    qcols,
    mom,
    rs_buf,
    tb,
    gz_buf,
    field,
    panel,
    send_h,
    recv_h,
    send_r,
    recv_r,
    send_g,
    recv_g,
    send_a,
    recv_a,
):
    zc, xc, slots, entries, channels, n_xy, n_gz = sizes
    atoms = zc * xc * slots
    layers = 2 * zc
    pairs = layers * channels
    share = 2 * channels // n_xy
    f32, bf16 = jnp.float32, jnp.bfloat16
    gz = lax.axis_index("gz")
    xy = lax.axis_index("xy")
    left, right = lax.rem(xy + n_xy - 1, n_xy), lax.rem(xy + 1, n_xy)
    xy_peers = [lax.rem(xy + d, n_xy) for d in range(1, n_xy)]
    gz_peers = [lax.rem(gz + d, n_gz) for d in range(1, n_gz)]
    has_below = gz > 0
    has_above = gz < n_gz - 1

    barrier = pltpu.get_barrier_semaphore()
    for peer in xy_peers:
        pl.semaphore_signal(barrier, inc=1, device_id={"xy": peer}, device_id_type=MESH)
    for peer in gz_peers:
        pl.semaphore_signal(barrier, inc=1, device_id={"gz": peer}, device_id_type=MESH)
    for present, step in ((has_below, -1), (has_above, 1)):

        @pl.when(present)
        def _():
            for side in (left, right):
                pl.semaphore_signal(
                    barrier, inc=1, device_id={"gz": gz + step, "xy": side}, device_id_type=MESH
                )

    cols = jnp.transpose(atom_rows[...])
    kinds = table.shape[0]
    onehot = cols[:, 0:1] == lax.broadcasted_iota(jnp.int32, (atoms, kinds), 1).astype(f32)
    hidden = (feat[...].astype(f32) + dot(onehot.astype(f32).astype(bf16), table[...])).astype(bf16)
    ext[1 : zc + 1, 1 : xc + 1] = hidden.reshape(zc, xc, slots, hidden.shape[1])

    @pl.when(jnp.logical_not(has_below))
    def _():
        ext[0] = jnp.zeros(ext.shape[1:], bf16)

    @pl.when(jnp.logical_not(has_above))
    def _():
        ext[zc + 1] = jnp.zeros(ext.shape[1:], bf16)

    diagonals = 2 * (has_below.astype(jnp.int32) + has_above.astype(jnp.int32))
    pl.semaphore_wait(barrier, n_xy - 1 + n_gz - 1 + diagonals)

    def remote(src, dst, send, recv, target):
        return pltpu.make_async_remote_copy(
            src_ref=src,
            dst_ref=dst,
            send_sem=send,
            recv_sem=recv,
            device_id=target,
            device_id_type=MESH,
        )

    x_copies = [
        remote(ext.at[pl.ds(1, zc), 1], ext.at[pl.ds(1, zc), xc + 1], send_h.at[0], recv_h.at[0], {"xy": left}),
        remote(ext.at[pl.ds(1, zc), xc], ext.at[pl.ds(1, zc), 0], send_h.at[1], recv_h.at[1], {"xy": right}),
    ]

    def z_copies(first, own, ghost, target):
        inner = pl.ds(1, xc)
        return [
            remote(ext.at[own, inner], ext.at[ghost, inner], send_h.at[first], recv_h.at[first], {"gz": target}),
            remote(ext.at[own, 1], ext.at[ghost, xc + 1], send_h.at[first + 1], recv_h.at[first + 1], {"gz": target, "xy": left}),
            remote(ext.at[own, xc], ext.at[ghost, 0], send_h.at[first + 2], recv_h.at[first + 2], {"gz": target, "xy": right}),
        ]

    down = z_copies(2, 1, zc + 1, gz - 1)
    rise = z_copies(5, zc, 0, gz + 1)
    for copy in x_copies:
        copy.start()

    @pl.when(has_below)
    def _():
        for copy in down:
            copy.start()

    @pl.when(has_above)
    def _():
        for copy in rise:
            copy.start()

    wide = 3 * pairs
    charges = dot(hidden, charge_cols[...]).astype(bf16)
    lane = lax.broadcasted_iota(jnp.int32, (atoms, wide), 1)
    row = lax.broadcasted_iota(jnp.int32, (atoms, 1), 0)
    layer = 2 * (row // (xc * slots)) + cols[:, 1:2].astype(jnp.int32)
    qcols[...] = jnp.where(layer == (lane % pairs) // channels, charges.astype(f32), 0.0).astype(bf16)

    cell_x = (xy * xc + (row // slots) % xc).astype(f32)
    coord_x = cell_width * cell_x + cols[:, 3:4]
    coord_y = cols[:, 4:5]
    step = 64
    for start in range(0, atoms, step):
        here = slice(start, start + step)
        at_x, at_y = coord_x[here], coord_y[here]
        sin_0, cos_0 = sincos(at_x * cst[0:1, :KX] + at_y * cst[1:2, :KX])
        ph[here, :KX] = cos_0.astype(bf16)
        ph[here, WAVES : WAVES + KX] = sin_0.astype(bf16)
        sin_x, cos_x = sincos(at_x * cst[3:4, :KX])
        sin_y, cos_y = sincos(at_y * cst[4:5, :KX])
        for b in range(1, len(BLOCKS)):
            cy, sy = cos_y[:, b - 1 : b], sin_y[:, b - 1 : b]
            ph[here, b * KX : (b + 1) * KX] = (cos_x * cy - sin_x * sy).astype(bf16)
            ph[here, WAVES + b * KX : WAVES + (b + 1) * KX] = (sin_x * cy + cos_x * sy).astype(bf16)

    moments = lax.dot_general(
        qcols[:, :pairs], ph[...], (((0,), (0,)), ((), ())), preferred_element_type=f32
    )
    for block in range(n_xy):
        p, c = divmod(block * share, channels)
        for l in range(layers):
            top = l * channels + c
            mom[block, l] = moments[top : top + share, p * WAVES : (p + 1) * WAVES]

    rs_copies = [
        remote(mom.at[peer], rs_buf.at[d], send_r.at[d], recv_r.at[d], {"xy": peer})
        for d, peer in enumerate(xy_peers)
    ]
    for copy in rs_copies:
        copy.start()

    d_all = dist[...]
    count = cols[:, 2:3].astype(jnp.int32)
    entry = lax.broadcasted_iota(jnp.int32, (atoms, entries), 1)
    usable = (entry < count) & (near[...] != 4 * slots + row % slots)
    ratio = d_all * (1.0 / cutoff)
    envelope = 1.0 - ratio * ratio
    wgt[...] = jnp.where(usable, envelope * envelope, 0.0)
    spacing = jnp.dot(d_all, spread[...], precision=lax.Precision.HIGHEST, preferred_element_type=f32)
    gap = spacing - centers[0:1, :]
    basis = jnp.exp(-(gap * gap)).astype(bf16)
    in_rows, in_cols = hidden_in.shape
    for part in range(basis.shape[1] // in_rows):
        for tile in range(in_cols // 256):
            pre = dot(basis[:, part * in_rows : (part + 1) * in_rows], hidden_in[:, tile * 256 : (tile + 1) * 256])
            first = part * in_cols + tile * 256
            fh[:, first : first + 256] = silu(pre).astype(bf16)

    for copy in rs_copies:
        copy.wait()
    total = mom[xy]
    for d in range(n_xy - 1):
        total = total + rs_buf[d]
    mine = [total[l] for l in range(layers)]

    def power(n):
        return cst[5 + n : 6 + n, :]

    tb[0] = sum(mine[l] * power(layers - 1 - l) for l in range(layers))
    tb[1] = sum(mine[l] * power(l) for l in range(layers))
    gz_copies = [
        remote(tb.at[jnp.where(peer > gz, 0, 1)], gz_buf.at[gz], send_g.at[d], recv_g.at[d], {"gz": peer})
        for d, peer in enumerate(gz_peers)
    ]
    for copy in gz_copies:
        copy.start()

    for copy in x_copies:
        copy.wait()

    @pl.when(has_below)
    def _():
        for copy in down:
            copy.wait_send()
        for copy in rise:
            copy.wait_recv()

    @pl.when(has_above)
    def _():
        for copy in rise:
            copy.wait_send()
        for copy in down:
            copy.wait_recv()

    width = feat.shape[1]
    codes = lax.broadcasted_iota(jnp.int32, (slots, 9 * slots), 1)

    def edge_row(z):
        def one(x, carry):
            base = pl.multiple_of((z * xc + x) * slots, slots)
            region = ext[z : z + 3, pl.ds(x, 3)].reshape(9 * slots, width)
            index = near[pl.ds(base, slots), :]
            chosen = jnp.concatenate(
                [
                    jnp.where(index[:, e : e + 1] == codes, 1.0, 0.0).astype(bf16)
                    for e in range(entries)
                ],
                axis=0,
            )
            gathered = dot(chosen, region)
            hid = fh[pl.ds(base, slots), :]
            both = jnp.concatenate(
                [hid[:, p * 128 : (p + 1) * 128] for p in range(hid.shape[1] // 128)], axis=0
            )
            filters = dot(both, hidden_out[...])
            weight = wgt[pl.ds(base, slots), :]
            acc = jnp.zeros((slots, width), f32)
            for e in range(entries):
                part = filters[(e // 2) * slots : (e // 2 + 1) * slots, (e % 2) * width : (e % 2 + 1) * width]
                acc = acc + weight[:, e : e + 1] * part * gathered[e * slots : (e + 1) * slots]
            agg[pl.ds(base, slots), :] = acc.astype(bf16)
            return carry

        lax.fori_loop(0, xc, one, 0)

    for z in range(zc // 2):
        edge_row(z)

    for copy in gz_copies:
        copy.wait()
    span = power(layers)
    blank = jnp.zeros(tb.shape[1:], f32)
    from_below = lax.fori_loop(0, gz, lambda t, s: s * span + gz_buf[t], blank)
    from_above = lax.fori_loop(
        0, n_gz - 1 - gz, lambda t, s: s * span + gz_buf[n_gz - 1 - t], blank
    )
    for l in range(layers):
        value = power(l + 1) * from_below + power(layers - l) * from_above
        for m in range(layers):
            value = value + power(abs(l - m)) * mine[m]
        field[xy, l] = value
    ag_copies = [
        remote(field.at[xy], field.at[xy], send_a.at[d], recv_a.at[d], {"xy": peer})
        for d, peer in enumerate(xy_peers)
    ]
    for copy in ag_copies:
        copy.start()

    for z in range(zc // 2, zc):
        edge_row(z)

    updated = silu(dot(agg[...], update_in[...])).astype(bf16)
    renewed = ext[1 : zc + 1, 1 : xc + 1].reshape(atoms, width).astype(f32) + dot(updated, update_out[...])
    out_feat[...] = renewed.astype(bf16)
    energy = jnp.sum(renewed * energy_w[0:1, :].astype(f32), axis=1, keepdims=True)

    for copy in ag_copies:
        copy.wait()
    wave_x, wave_y, wave_w = cst[0:1, :], cst[1:2, :], cst[2:3, :]
    half = n_xy // 2
    for l in range(layers):
        f_cos = jnp.concatenate([field[b, l] for b in range(half)], axis=0) * wave_w
        f_sin = jnp.concatenate([field[half + b, l] for b in range(half)], axis=0) * wave_w
        lines = ((f_cos, f_sin), (wave_x * f_sin, -wave_x * f_cos), (wave_y * f_sin, -wave_y * f_cos))
        for r, (cos_part, sin_part) in enumerate(lines):
            top = r * pairs + l * channels
            panel[top : top + channels, :WAVES] = cos_part.astype(bf16)
            panel[top : top + channels, WAVES:] = sin_part.astype(bf16)
    evaluated = lax.dot_general(
        ph[...], panel[...], (((1,), (1,)), ((), ())), preferred_element_type=f32
    )
    product = evaluated * qcols[...].astype(f32)
    group = lane // pairs
    sums = [
        jnp.sum(jnp.where(group == r, product, 0.0), axis=1, keepdims=True) for r in range(3)
    ]
    narrow = lax.broadcasted_iota(jnp.int32, (atoms, 128), 1)
    packed = jnp.where(
        narrow == 0, energy + 0.5 * sums[0], jnp.where(narrow == 1, -sums[1], -sums[2])
    )
    out_rows[...] = jnp.transpose(packed)[:8]


def shards(
    n_xy,
    n_gz,
    features,
    species,
    sublayer,
    offsets,
    neighbours,
    neighbour_count,
    distances,
    species_table,
    charge_weight,
    radial_in,
    radial_out,
    update_in,
    update_out,
    energy_weight,
):
    f32, bf16 = jnp.float32, jnp.bfloat16
    zc, xc, slots, width = features.shape
    entries = neighbours.shape[3]
    channels = charge_weight.shape[1]
    atoms = zc * xc * slots
    layers = 2 * zc
    basis_count, radial = radial_in.shape
    share = 2 * channels // n_xy
    cst = wave_constants(cell_width * (xc * n_xy), layers)
    spread = np.kron(np.eye(entries), np.ones((1, basis_count))).astype(np.float32)
    mids = np.float32(cutoff) * np.arange(basis_count).astype(np.float32) / np.float32(basis_count - 1)
    centers = np.tile(mids, (8, entries)).astype(np.float32)
    flat = [species, sublayer, neighbour_count, offsets[0], offsets[1]]
    atom_rows = jnp.stack([a.reshape(atoms).astype(f32) for a in flat] + [jnp.zeros((atoms,), f32)] * 3)
    group = 128 // basis_count
    hidden_in = jnp.kron(jnp.eye(group, dtype=bf16), radial_in)
    hidden_out = jnp.kron(jnp.eye(128 // radial, dtype=bf16), radial_out)
    charge_cols = jnp.tile(charge_weight, (1, 3 * layers))
    sizes = (zc, xc, slots, entries, channels, n_xy, n_gz)
    dma = pltpu.SemaphoreType.DMA
    vmem = pl.BlockSpec(memory_space=pltpu.VMEM)
    out_feat, out_rows = pl.pallas_call(
        functools.partial(kernel, sizes),
        out_shape=(
            jax.ShapeDtypeStruct((atoms, width), bf16),
            jax.ShapeDtypeStruct((8, atoms), f32),
        ),
        in_specs=[vmem] * 14,
        out_specs=(vmem, vmem),
        scratch_shapes=[
            pltpu.VMEM((zc + 2, xc + 2, slots, width), bf16),
            pltpu.VMEM((atoms, 2 * WAVES), bf16),
            pltpu.VMEM((atoms, entries * radial), bf16),
            pltpu.VMEM((atoms, entries), f32),
            pltpu.VMEM((atoms, width), bf16),
            pltpu.VMEM((atoms, 3 * layers * channels), bf16),
            pltpu.VMEM((n_xy, layers, share, WAVES), f32),
            pltpu.VMEM((n_xy - 1, layers, share, WAVES), f32),
            pltpu.VMEM((2, share, WAVES), f32),
            pltpu.VMEM((n_gz, share, WAVES), f32),
            pltpu.VMEM((n_xy, layers, share, WAVES), f32),
            pltpu.VMEM((3 * layers * channels, 2 * WAVES), bf16),
            dma((8,)),
            dma((8,)),
            dma((n_xy - 1,)),
            dma((n_xy - 1,)),
            dma((n_gz - 1,)),
            dma((n_gz - 1,)),
            dma((n_xy - 1,)),
            dma((n_xy - 1,)),
        ],
        compiler_params=pltpu.CompilerParams(
            collective_id=0, has_side_effects=True, vmem_limit_bytes=40 * 1024 * 1024
        ),
        cost_estimate=pl.CostEstimate(flops=2_000_000_000, bytes_accessed=2_000_000, transcendentals=2_000_000),
    )(
        features.reshape(atoms, width),
        atom_rows,
        neighbours.reshape(atoms, entries),
        distances.reshape(atoms, entries),
        species_table,
        charge_cols,
        hidden_in,
        hidden_out,
        update_in,
        update_out,
        energy_weight.reshape(1, width),
        jnp.asarray(cst),
        jnp.asarray(spread),
        jnp.asarray(centers),
    )
    return (
        out_feat.reshape(features.shape),
        out_rows[0].reshape(zc, xc, slots),
        out_rows[1:3].reshape(2, zc, xc, slots),
    )


def solution(mesh):
    atom = P(("groups", "gz"), "xy", None)
    atom_wide = P(("groups", "gz"), "xy", None, None)
    pair = P(None, ("groups", "gz"), "xy", None)
    in_specs = (atom_wide, atom, atom, pair, atom_wide, atom, atom_wide) + (P(),) * 7
    body = functools.partial(shards, mesh.shape["xy"], mesh.shape["gz"])
    return jax.shard_map(
        body, mesh=mesh, in_specs=in_specs, out_specs=(atom_wide, atom, pair), check_vma=False
    )
```

```python
import functools
import math

import jax
import jax.numpy as jnp
import numpy as np
from jax import lax
from jax.experimental import pallas as pl
from jax.experimental.pallas import tpu as pltpu
from jax.sharding import PartitionSpec as P

KX = 128
KY = 8
MESH = pl.DeviceIdType.MESH

cell_width = 11.0
layer_depth = 5.5
screening = 0.025
smearing = 1.0
coupling = 0.25
cutoff = 8.0

BLOCKS = (4, 0, 5, 6, 7)
LANES = 384


def wave_constants(width_x, layers, n_xy):
    f32 = np.float32
    per = KX // n_xy

    def factors(index_x, index_y, count):
        wave_x = f32(2.0 * math.pi / width_x) * (index_x - KX // 2).astype(f32)
        wave_y = f32(2.0 * math.pi / cell_width) * (index_y - KY // 2).astype(f32)
        square = wave_x * wave_x + wave_y * wave_y
        screened = np.sqrt(square + f32(screening * screening))
        weight = f32(coupling * (2.0 * math.pi / (width_x * cell_width))) * np.exp(
            f32(-0.5 * smearing * smearing) * square
        )
        return wave_x, wave_y, weight / screened * count, screened

    strips = []
    for strip in range(n_xy):
        own = np.arange(strip * per, (strip + 1) * per)
        index_x = np.tile(own, len(BLOCKS) - 1)
        index_y = np.repeat(np.array(BLOCKS[1:]), per)
        count = np.where((index_y > KY // 2) & (index_x > 0), 2.0, 1.0).astype(f32)
        part_a = factors(index_x, index_y, count)
        index_x, index_y = own.copy(), np.full(per, KY // 2)
        count = np.where((own > 0) & (own < KX // 2), 2.0, 1.0).astype(f32)
        count[own > KX // 2] = 0.0
        for spare, j in enumerate((1, 2, 3)):
            place = KX // 2 + 1 + spare
            count[own == place] = 1.0
            index_y[own == place] = j
            index_x[own == place] = 0
        part_b = factors(index_x, index_y, count)
        lanes = []
        for one, two in zip(part_a, part_b):
            one = np.pad(one, (0, 128 - one.size))
            two = np.pad(two, (0, 64 - two.size))
            lanes.append(np.concatenate([one, one, two, two]))
        wave_x, wave_y, weight, screened = lanes
        sign = np.repeat(np.array([1, -1, 1, -1], f32), [128, 128, 64, 64])
        powers = [np.exp(-screened * f32(layer_depth) * f32(n)) for n in range(layers + 1)]
        rows = [wave_x, wave_y, weight, sign * wave_x, sign * wave_y] + powers
        rows += [np.zeros(LANES, f32)] * (-len(rows) % 8)
        strips.append(np.stack(rows))
    return np.stack(strips).astype(f32)


def reduced(angle):
    turns = jnp.floor(angle * (2.0 / math.pi) + 0.5)
    rest = angle - turns * 1.5703125
    rest = rest - turns * 4.8375129699707031e-4
    rest = rest - turns * 7.5497899548918822e-8
    square = rest * rest
    sine = rest + rest * square * (
        (-1.9515295891e-4 * square + 8.3321608736e-3) * square - 1.6666654611e-1
    )
    cosine = (1.0 - 0.5 * square) + square * square * (
        (2.443315711809948e-5 * square - 1.388731625493765e-3) * square + 4.166664568298827e-2
    )
    return turns.astype(jnp.int32), sine, cosine


def at_quadrant(quadrant, sine, cosine):
    value = jnp.where((quadrant & 1) == 1, cosine, sine)
    return jnp.where((quadrant & 2) == 2, -value, value)


def silu(value):
    half = 0.5 * value
    return half + half * jnp.tanh(half)


def dot(a, b):
    return jnp.dot(a, b, preferred_element_type=jnp.float32)


def kernel(
    sizes,
    feat,
    species,
    sublayer,
    counts,
    offsets,
    near,
    dist,
    table,
    charge_w,
    radial_in,
    radial_out,
    update_in,
    update_out,
    energy_w,
    cst,
    centers,
    out_feat,
    out_energy,
    out_forces,
    ext,
    ph,
    fh,
    wgt,
    agg,
    own_rows,
    coords,
    q_all,
    qw,
    tb,
    gz_buf,
    mine,
    panel,
    part,
    part_buf,
    send_h,
    recv_h,
    send_c,
    recv_c,
    send_q,
    recv_q,
    send_g,
    recv_g,
    send_p,
    recv_p,
):
    zc, xc, slots, entries, channels, n_xy, n_gz = sizes
    cells = zc * xc
    atoms = cells * slots
    layers = 2 * zc
    pairs = layers * channels
    f32, bf16, i32 = jnp.float32, jnp.bfloat16, jnp.int32
    exact = lax.Precision.HIGHEST
    iota = lax.broadcasted_iota
    width = feat.shape[1]
    gz = lax.axis_index("gz")
    xy = lax.axis_index("xy")
    left, right = lax.rem(xy + n_xy - 1, n_xy), lax.rem(xy + 1, n_xy)
    xy_peers = [lax.rem(xy + d, n_xy) for d in range(1, n_xy)]
    gz_peers = [lax.rem(gz + d, n_gz) for d in range(1, n_gz)]
    has_below = gz > 0
    has_above = gz < n_gz - 1

    barrier = pltpu.get_barrier_semaphore()
    for peer in xy_peers:
        pl.semaphore_signal(barrier, inc=1, device_id={"xy": peer}, device_id_type=MESH)
    for peer in gz_peers:
        pl.semaphore_signal(barrier, inc=1, device_id={"gz": peer}, device_id_type=MESH)
    for present, step in ((has_below, -1), (has_above, 1)):

        @pl.when(present)
        def _():
            for side in (left, right):
                pl.semaphore_signal(
                    barrier, inc=1, device_id={"gz": gz + step, "xy": side}, device_id_type=MESH
                )

    unfold = (iota(i32, (slots, atoms), 1) % slots == iota(i32, (slots, atoms), 0)).astype(f32)
    own_cell = iota(i32, (cells, atoms), 1) // slots == iota(i32, (cells, atoms), 0)
    stacked = jnp.concatenate(
        [species[...].astype(f32), sublayer[...].astype(f32), counts[...].astype(f32), offsets[...]],
        axis=0,
    )
    wide = jnp.dot(stacked, unfold, precision=exact, preferred_element_type=f32)
    kind_row, sub_row, count_row, x_row, y_row = [
        jnp.sum(jnp.where(own_cell, wide[i * cells : (i + 1) * cells], 0.0), axis=0, keepdims=True)
        for i in range(5)
    ]
    atom_cell = iota(i32, (1, atoms), 1) // slots
    x_row = cell_width * (xy * xc + atom_cell % xc).astype(f32) + x_row
    layer_row = sub_row + (2 * (atom_cell // xc)).astype(f32)
    blank = jnp.zeros((3, atoms), f32)
    rows = jnp.concatenate([x_row, y_row, layer_row, kind_row, count_row, blank], axis=0)
    coords[xy] = rows
    cols = jnp.transpose(rows)

    kinds = table.shape[0]
    onehot = cols[:, 3:4] == iota(i32, (atoms, kinds), 1).astype(f32)
    hidden = (feat[...].astype(f32) + dot(onehot.astype(f32).astype(bf16), table[...])).astype(bf16)
    ext[1 : zc + 1, 1 : xc + 1] = hidden.reshape(zc, xc, slots, width)
    q_all[xy] = lax.dot_general(
        charge_w[...], hidden, (((1,), (1,)), ((), ())), preferred_element_type=f32
    ).astype(bf16)

    @pl.when(jnp.logical_not(has_below))
    def _():
        ext[0] = jnp.zeros(ext.shape[1:], bf16)

    @pl.when(jnp.logical_not(has_above))
    def _():
        ext[zc + 1] = jnp.zeros(ext.shape[1:], bf16)

    diagonals = 2 * (has_below.astype(i32) + has_above.astype(i32))
    pl.semaphore_wait(barrier, n_xy - 1 + n_gz - 1 + diagonals)

    def remote(src, dst, send, recv, target):
        return pltpu.make_async_remote_copy(
            src_ref=src,
            dst_ref=dst,
            send_sem=send,
            recv_sem=recv,
            device_id=target,
            device_id_type=MESH,
        )

    strip_copies = []
    for d, peer in enumerate(xy_peers):
        strip_copies += [
            remote(coords.at[xy], coords.at[xy], send_c.at[d], recv_c.at[d], {"xy": peer}),
            remote(q_all.at[xy], q_all.at[xy], send_q.at[d], recv_q.at[d], {"xy": peer}),
        ]
    for copy in strip_copies:
        copy.start()

    inner = pl.ds(1, zc)
    x_copies = [
        remote(ext.at[inner, 1], ext.at[inner, xc + 1], send_h.at[0], recv_h.at[0], {"xy": left}),
        remote(ext.at[inner, xc], ext.at[inner, 0], send_h.at[1], recv_h.at[1], {"xy": right}),
    ]

    def z_copies(first, own, ghost, target):
        strip = pl.ds(1, xc)
        return [
            remote(ext.at[own, strip], ext.at[ghost, strip], send_h.at[first], recv_h.at[first], {"gz": target}),
            remote(ext.at[own, 1], ext.at[ghost, xc + 1], send_h.at[first + 1], recv_h.at[first + 1], {"gz": target, "xy": left}),
            remote(ext.at[own, xc], ext.at[ghost, 0], send_h.at[first + 2], recv_h.at[first + 2], {"gz": target, "xy": right}),
        ]

    down = z_copies(2, 1, zc + 1, gz - 1)
    rise = z_copies(5, zc, 0, gz + 1)
    for copy in x_copies:
        copy.start()

    @pl.when(has_below)
    def _():
        for copy in down:
            copy.start()

    @pl.when(has_above)
    def _():
        for copy in rise:
            copy.start()

    def strip_phases(strip):
        at = jnp.transpose(coords[strip])
        turn = jnp.where(iota(i32, (1, 128), 1) < 64, 1, 0)
        step = 64
        for start in range(0, atoms, step):
            here = slice(start, start + step)
            at_x, at_y = at[here, 0:1], at[here, 1:2]
            lines = pl.ds(strip * atoms + start, step)
            quadrant, sine, cosine = reduced(at_x * cst[xy, 0:1, :128] + at_y * cst[xy, 1:2, :128])
            ph[lines, :128] = at_quadrant(quadrant + 1, sine, cosine).astype(bf16)
            ph[lines, 128:256] = at_quadrant(quadrant, sine, cosine).astype(bf16)
            quadrant, sine, cosine = reduced(at_x * cst[xy, 0:1, 256:] + at_y * cst[xy, 1:2, 256:])
            ph[lines, 256:] = at_quadrant(quadrant + turn, sine, cosine).astype(bf16)

    def strip_moments(strip):
        layer = coords[strip][2:3]
        charges = q_all[strip].astype(f32)
        weighted = jnp.concatenate(
            [jnp.where(layer == float(l), charges, 0.0) for l in range(layers)], axis=0
        ).astype(bf16)
        qw[strip] = weighted
        return dot(weighted, ph[pl.ds(strip * atoms, atoms), :])

    strip_phases(xy)
    total = strip_moments(xy)

    d_all = dist[...]
    slot = iota(i32, (atoms, 1), 0) % slots
    entry = iota(i32, (atoms, entries), 1)
    usable = (entry < cols[:, 4:5].astype(i32)) & (near[...] != 4 * slots + slot)
    ratio = d_all * (1.0 / cutoff)
    envelope = 1.0 - ratio * ratio
    wgt[...] = jnp.where(usable, envelope * envelope, 0.0)
    basis_count, radial = radial_in.shape
    spread_shape = (entries, entries * basis_count)
    spread = (iota(i32, spread_shape, 1) // basis_count == iota(i32, spread_shape, 0)).astype(f32)
    spacing = jnp.dot(d_all, spread, precision=exact, preferred_element_type=f32)
    gap = spacing - centers[0:1, :]
    basis = jnp.exp(-(gap * gap)).astype(bf16)
    group = 128 // basis_count
    tall = jnp.concatenate([radial_in[...].astype(f32)] * group, axis=0)
    flat = jnp.concatenate([tall] * group, axis=1)
    diagonal = iota(i32, flat.shape, 0) // basis_count == iota(i32, flat.shape, 1) // radial
    hidden_in = jnp.where(diagonal, flat, 0.0).astype(bf16)
    for block in range(entries // group):
        for tile in range(flat.shape[1] // 256):
            pre = dot(basis[:, block * 128 : (block + 1) * 128], hidden_in[:, tile * 256 : (tile + 1) * 256])
            first = block * flat.shape[1] + tile * 256
            fh[:, first : first + 256] = silu(pre).astype(bf16)
    pack = 128 // radial
    tall = jnp.concatenate([radial_out[...].astype(f32)] * pack, axis=0)
    flat = jnp.concatenate([tall] * pack, axis=1)
    diagonal = iota(i32, flat.shape, 0) // radial == iota(i32, flat.shape, 1) // width
    hidden_out = jnp.where(diagonal, flat, 0.0).astype(bf16)

    for copy in strip_copies:
        copy.wait()

    def add_strip(d, total):
        strip = lax.rem(xy + d, n_xy)
        strip_phases(strip)
        return total + strip_moments(strip)

    total = lax.fori_loop(1, n_xy, add_strip, total)
    mine[...] = total

    def power(n):
        return cst[xy, 5 + n : 6 + n, :]

    def layer_moments(l):
        return mine[l * channels : (l + 1) * channels, :]

    tb[0] = sum(layer_moments(l) * power(layers - 1 - l) for l in range(layers))
    tb[1] = sum(layer_moments(l) * power(l) for l in range(layers))
    gz_copies = [
        remote(tb.at[jnp.where(peer > gz, 0, 1)], gz_buf.at[gz], send_g.at[d], recv_g.at[d], {"gz": peer})
        for d, peer in enumerate(gz_peers)
    ]
    for copy in gz_copies:
        copy.start()

    for copy in x_copies:
        copy.wait()

    @pl.when(has_below)
    def _():
        for copy in down:
            copy.wait_send()
        for copy in rise:
            copy.wait_recv()

    @pl.when(has_above)
    def _():
        for copy in rise:
            copy.wait_send()
        for copy in down:
            copy.wait_recv()

    codes = iota(i32, (slots, 9 * slots), 1)

    def edge_row(z):
        def one(x, carry):
            base = pl.multiple_of((z * xc + x) * slots, slots)
            region = ext[z : z + 3, pl.ds(x, 3)].reshape(9 * slots, width)
            index = near[pl.ds(base, slots), :]
            chosen = jnp.concatenate(
                [
                    jnp.where(index[:, e : e + 1] == codes, 1.0, 0.0).astype(bf16)
                    for e in range(entries)
                ],
                axis=0,
            )
            gathered = dot(chosen, region)
            hid = fh[pl.ds(base, slots), :]
            both = jnp.concatenate(
                [hid[:, p * 128 : (p + 1) * 128] for p in range(hid.shape[1] // 128)], axis=0
            )
            filters = dot(both, hidden_out)
            weight = wgt[pl.ds(base, slots), :]
            acc = jnp.zeros((slots, width), f32)
            for e in range(entries):
                row, col = (e // pack) * slots, (e % pack) * width
                filtered = weight[:, e : e + 1] * filters[row : row + slots, col : col + width]
                acc = acc + filtered * gathered[e * slots : (e + 1) * slots]
            agg[pl.ds(base, slots), :] = acc.astype(bf16)
            return carry

        lax.fori_loop(0, xc, one, 0)

    for z in range(zc // 2):
        edge_row(z)

    for copy in gz_copies:
        copy.wait()
    span = power(layers)
    none = jnp.zeros(tb.shape[1:], f32)
    from_below = lax.fori_loop(0, gz, lambda t, s: s * span + gz_buf[t], none)
    from_above = lax.fori_loop(0, n_gz - 1 - gz, lambda t, s: s * span + gz_buf[n_gz - 1 - t], none)
    for l in range(layers):
        value = power(l + 1) * from_below + power(layers - l) * from_above
        for m in range(layers):
            value = value + power(abs(l - m)) * layer_moments(m)
        value = value * cst[xy, 2:3, :]
        swapped = jnp.concatenate(
            [value[:, 128:256], value[:, :128], value[:, 320:], value[:, 256:320]], axis=1
        )
        lines = (value, cst[xy, 3:4, :] * swapped, cst[xy, 4:5, :] * swapped)
        for r, line in enumerate(lines):
            top = r * pairs + l * channels
            panel[top : top + channels, :] = line.astype(bf16)

    def strip_sums(strip):
        evaluated = lax.dot_general(
            panel[...],
            ph[pl.ds(strip * atoms, atoms), :],
            (((1,), (1,)), ((), ())),
            preferred_element_type=f32,
        )
        charges = qw[strip].astype(f32)
        lines = [
            jnp.sum(evaluated[r * pairs : (r + 1) * pairs] * charges, axis=0, keepdims=True)
            for r in range(3)
        ]
        return jnp.concatenate(lines + [jnp.zeros((5, atoms), f32)], axis=0)

    part_copies = []
    for d, peer in enumerate(xy_peers):
        part[d] = strip_sums(peer)
        copy = remote(part.at[d], part_buf.at[d], send_p.at[d], recv_p.at[d], {"xy": peer})
        copy.start()
        part_copies.append(copy)
    own_rows[...] = strip_sums(xy)

    for z in range(zc // 2, zc):
        edge_row(z)

    updated = silu(dot(agg[...], update_in[...])).astype(bf16)
    renewed = ext[1 : zc + 1, 1 : xc + 1].reshape(atoms, width).astype(f32) + dot(updated, update_out[...])
    out_feat[...] = renewed.astype(bf16)
    readout = jnp.broadcast_to(energy_w[0:1, :].astype(f32), (8, width))
    energy = lax.dot_general(
        readout, renewed, (((1,), (1,)), ((), ())), precision=exact, preferred_element_type=f32
    )

    for copy in part_copies:
        copy.wait()
    sums = own_rows[...]
    for d in range(n_xy - 1):
        sums = sums + part_buf[d]
    finals = (energy[0:1] + 0.5 * sums[0:1], -sums[1:2], -sums[2:3])
    spread_out = jnp.concatenate([jnp.where(own_cell, line, 0.0) for line in finals], axis=0)
    folded = lax.dot_general(
        spread_out, unfold, (((1,), (1,)), ((), ())), precision=exact, preferred_element_type=f32
    )
    out_energy[...] = folded[:cells]
    out_forces[...] = folded[cells:]


def shards(
    n_xy,
    n_gz,
    features,
    species,
    sublayer,
    offsets,
    neighbours,
    neighbour_count,
    distances,
    species_table,
    charge_weight,
    radial_in,
    radial_out,
    update_in,
    update_out,
    energy_weight,
):
    f32, bf16 = jnp.float32, jnp.bfloat16
    zc, xc, slots, width = features.shape
    entries = neighbours.shape[3]
    channels = charge_weight.shape[1]
    cells = zc * xc
    atoms = cells * slots
    layers = 2 * zc
    pairs = layers * channels
    basis_count, radial = radial_in.shape
    cst = wave_constants(cell_width * (xc * n_xy), layers, n_xy)
    mids = np.float32(cutoff) * np.arange(basis_count).astype(np.float32) / np.float32(basis_count - 1)
    centers = np.tile(mids, (8, entries)).astype(np.float32)
    sizes = (zc, xc, slots, entries, channels, n_xy, n_gz)
    dma = pltpu.SemaphoreType.DMA
    vmem = pl.BlockSpec(memory_space=pltpu.VMEM)
    out_feat, energy, forces = pl.pallas_call(
        functools.partial(kernel, sizes),
        out_shape=(
            jax.ShapeDtypeStruct((atoms, width), bf16),
            jax.ShapeDtypeStruct((cells, slots), f32),
            jax.ShapeDtypeStruct((2 * cells, slots), f32),
        ),
        in_specs=[vmem] * 16,
        out_specs=(vmem, vmem, vmem),
        scratch_shapes=[
            pltpu.VMEM((zc + 2, xc + 2, slots, width), bf16),
            pltpu.VMEM((n_xy * atoms, LANES), bf16),
            pltpu.VMEM((atoms, entries * radial), bf16),
            pltpu.VMEM((atoms, entries), f32),
            pltpu.VMEM((atoms, width), bf16),
            pltpu.VMEM((8, atoms), f32),
            pltpu.VMEM((n_xy, 8, atoms), f32),
            pltpu.VMEM((n_xy, channels, atoms), bf16),
            pltpu.VMEM((n_xy, pairs, atoms), bf16),
            pltpu.VMEM((2, channels, LANES), f32),
            pltpu.VMEM((n_gz, channels, LANES), f32),
            pltpu.VMEM((pairs, LANES), f32),
            pltpu.VMEM((3 * pairs, LANES), bf16),
            pltpu.VMEM((n_xy - 1, 8, atoms), f32),
            pltpu.VMEM((n_xy - 1, 8, atoms), f32),
            dma((8,)),
            dma((8,)),
            dma((n_xy - 1,)),
            dma((n_xy - 1,)),
            dma((n_xy - 1,)),
            dma((n_xy - 1,)),
            dma((n_gz - 1,)),
            dma((n_gz - 1,)),
            dma((n_xy - 1,)),
            dma((n_xy - 1,)),
        ],
        compiler_params=pltpu.CompilerParams(
            collective_id=0, has_side_effects=True, vmem_limit_bytes=40 * 1024 * 1024
        ),
        cost_estimate=pl.CostEstimate(flops=2_000_000_000, bytes_accessed=2_000_000, transcendentals=2_000_000),
    )(
        features.reshape(atoms, width),
        species.reshape(cells, slots),
        sublayer.reshape(cells, slots),
        neighbour_count.reshape(cells, slots),
        offsets.reshape(2 * cells, slots),
        neighbours.reshape(atoms, entries),
        distances.reshape(atoms, entries),
        species_table,
        charge_weight.T,
        radial_in,
        radial_out,
        update_in,
        update_out,
        energy_weight.reshape(1, width),
        jnp.asarray(cst),
        jnp.asarray(centers),
    )
    return (
        out_feat.reshape(features.shape),
        energy.reshape(species.shape),
        forces.reshape((2,) + species.shape),
    )


def solution(mesh):
    atom = P(("groups", "gz"), "xy", None)
    atom_wide = P(("groups", "gz"), "xy", None, None)
    pair = P(None, ("groups", "gz"), "xy", None)
    in_specs = (atom_wide, atom, atom, pair, atom_wide, atom, atom_wide) + (P(),) * 7
    body = functools.partial(shards, mesh.shape["xy"], mesh.shape["gz"])
    return jax.shard_map(
        body, mesh=mesh, in_specs=in_specs, out_specs=(atom_wide, atom, pair), check_vma=False
    )
```

```python
import functools
import math

import jax
import jax.numpy as jnp
import numpy as np
from jax import lax
from jax.experimental import pallas as pl
from jax.experimental.pallas import tpu as pltpu
from jax.sharding import PartitionSpec as P

KX = 128
KY = 8
MESH = pl.DeviceIdType.MESH

cell_width = 11.0
layer_depth = 5.5
screening = 0.025
smearing = 1.0
coupling = 0.25
cutoff = 8.0

BLOCKS = (4, 0, 5, 6, 7)
LANES = 384


def wave_constants(width_x, layers, n_xy):
    f32 = np.float32
    per = KX // n_xy

    def factors(index_x, index_y, count):
        wave_x = f32(2.0 * math.pi / width_x) * (index_x - KX // 2).astype(f32)
        wave_y = f32(2.0 * math.pi / cell_width) * (index_y - KY // 2).astype(f32)
        square = wave_x * wave_x + wave_y * wave_y
        screened = np.sqrt(square + f32(screening * screening))
        weight = f32(coupling * (2.0 * math.pi / (width_x * cell_width))) * np.exp(
            f32(-0.5 * smearing * smearing) * square
        )
        return wave_x, wave_y, weight / screened * count, screened

    strips = []
    for strip in range(n_xy):
        own = np.arange(strip * per, (strip + 1) * per)
        index_x = np.tile(own, len(BLOCKS) - 1)
        index_y = np.repeat(np.array(BLOCKS[1:]), per)
        count = np.where((index_y > KY // 2) & (index_x > 0), 2.0, 1.0).astype(f32)
        part_a = factors(index_x, index_y, count)
        index_x, index_y = own.copy(), np.full(per, KY // 2)
        count = np.where((own > 0) & (own < KX // 2), 2.0, 1.0).astype(f32)
        count[own > KX // 2] = 0.0
        for spare, j in enumerate((1, 2, 3)):
            place = KX // 2 + 1 + spare
            count[own == place] = 1.0
            index_y[own == place] = j
            index_x[own == place] = 0
        part_b = factors(index_x, index_y, count)
        lanes = []
        for one, two in zip(part_a, part_b):
            one = np.pad(one, (0, 128 - one.size))
            two = np.pad(two, (0, 64 - two.size))
            lanes.append(np.concatenate([one, one, two, two]))
        wave_x, wave_y, weight, screened = lanes
        sign = np.repeat(np.array([1, -1, 1, -1], f32), [128, 128, 64, 64])
        powers = [np.exp(-screened * f32(layer_depth) * f32(n)) for n in range(layers + 1)]
        rows = [wave_x, wave_y, weight, sign * wave_x, sign * wave_y] + powers
        rows += [np.zeros(LANES, f32)] * (-len(rows) % 8)
        strips.append(np.stack(rows))
    return np.stack(strips).astype(f32)


def reduced(angle):
    turns = jnp.floor(angle * (2.0 / math.pi) + 0.5)
    rest = angle - turns * 1.5703125
    rest = rest - turns * 4.8375129699707031e-4
    rest = rest - turns * 7.5497899548918822e-8
    square = rest * rest
    sine = rest + rest * square * (
        (-1.9515295891e-4 * square + 8.3321608736e-3) * square - 1.6666654611e-1
    )
    cosine = (1.0 - 0.5 * square) + square * square * (
        (2.443315711809948e-5 * square - 1.388731625493765e-3) * square + 4.166664568298827e-2
    )
    return turns.astype(jnp.int32), sine, cosine


def at_quadrant(quadrant, sine, cosine):
    value = jnp.where((quadrant & 1) == 1, cosine, sine)
    return jnp.where((quadrant & 2) == 2, -value, value)


def silu(value):
    half = 0.5 * value
    return half + half * jnp.tanh(half)


def dot(a, b):
    return jnp.dot(a, b, preferred_element_type=jnp.float32)


INPUTS = 16


def writer(feat_in, energy_in, forces_in, feat_out, energy_out, forces_out, sems):
    pairs = ((feat_in, feat_out), (energy_in, energy_out), (forces_in, forces_out))
    copies = [pltpu.make_async_copy(a, b, sems.at[i]) for i, (a, b) in enumerate(pairs)]
    for copy in copies:
        copy.start()
    for copy in copies:
        copy.wait()


def kernel(sizes, *refs):
    in_hbm, refs = refs[:INPUTS], refs[INPUTS:]
    (out_feat, out_energy, out_forces), refs = refs[:3], refs[3:]
    held, refs = refs[:INPUTS], refs[INPUTS:]
    (
        load_sem,
        ext,
        ph,
        fh,
        wgt,
        agg,
        own_rows,
        coords,
        q_all,
        qw,
        tb,
        gz_buf,
        mine,
        panel,
        part,
        part_buf,
        send_h,
        recv_h,
        send_c,
        recv_c,
        send_q,
        recv_q,
        send_g,
        recv_g,
        send_p,
        recv_p,
    ) = refs
    (
        species,
        sublayer,
        counts,
        offsets,
        feat,
        table,
        charge_w,
        cst,
        dist,
        near,
        centers,
        radial_in,
        radial_out,
        update_in,
        update_out,
        energy_w,
    ) = held
    loads = [
        pltpu.make_async_copy(a, b, load_sem.at[i]) for i, (a, b) in enumerate(zip(in_hbm, held))
    ]
    for load in loads:
        load.start()
    zc, xc, slots, entries, channels, n_xy, n_gz = sizes
    cells = zc * xc
    atoms = cells * slots
    layers = 2 * zc
    pairs = layers * channels
    f32, bf16, i32 = jnp.float32, jnp.bfloat16, jnp.int32
    exact = lax.Precision.HIGHEST
    iota = lax.broadcasted_iota
    width = feat.shape[1]
    gz = lax.axis_index("gz")
    xy = lax.axis_index("xy")
    left, right = lax.rem(xy + n_xy - 1, n_xy), lax.rem(xy + 1, n_xy)
    xy_peers = [lax.rem(xy + d, n_xy) for d in range(1, n_xy)]
    gz_peers = [lax.rem(gz + d, n_gz) for d in range(1, n_gz)]
    has_below = gz > 0
    has_above = gz < n_gz - 1

    barrier = pltpu.get_barrier_semaphore()
    for peer in xy_peers:
        pl.semaphore_signal(barrier, inc=1, device_id={"xy": peer}, device_id_type=MESH)
    for peer in gz_peers:
        pl.semaphore_signal(barrier, inc=1, device_id={"gz": peer}, device_id_type=MESH)
    for present, step in ((has_below, -1), (has_above, 1)):

        @pl.when(present)
        def _():
            for side in (left, right):
                pl.semaphore_signal(
                    barrier, inc=1, device_id={"gz": gz + step, "xy": side}, device_id_type=MESH
                )

    for load in loads[:4]:
        load.wait()
    unfold = (iota(i32, (slots, atoms), 1) % slots == iota(i32, (slots, atoms), 0)).astype(f32)
    own_cell = iota(i32, (cells, atoms), 1) // slots == iota(i32, (cells, atoms), 0)
    stacked = jnp.concatenate(
        [species[...].astype(f32), sublayer[...].astype(f32), counts[...].astype(f32), offsets[...]],
        axis=0,
    )
    wide = jnp.dot(stacked, unfold, precision=exact, preferred_element_type=f32)
    kind_row, sub_row, count_row, x_row, y_row = [
        jnp.sum(jnp.where(own_cell, wide[i * cells : (i + 1) * cells], 0.0), axis=0, keepdims=True)
        for i in range(5)
    ]
    atom_cell = iota(i32, (1, atoms), 1) // slots
    x_row = cell_width * (xy * xc + atom_cell % xc).astype(f32) + x_row
    layer_row = sub_row + (2 * (atom_cell // xc)).astype(f32)
    blank = jnp.zeros((3, atoms), f32)
    rows = jnp.concatenate([x_row, y_row, layer_row, kind_row, count_row, blank], axis=0)
    coords[xy] = rows
    cols = jnp.transpose(rows)

    for load in loads[4:7]:
        load.wait()
    kinds = table.shape[0]
    onehot = cols[:, 3:4] == iota(i32, (atoms, kinds), 1).astype(f32)
    hidden = (feat[...].astype(f32) + dot(onehot.astype(f32).astype(bf16), table[...])).astype(bf16)
    ext[1 : zc + 1, 1 : xc + 1] = hidden.reshape(zc, xc, slots, width)
    q_all[xy] = lax.dot_general(
        charge_w[...], hidden, (((1,), (1,)), ((), ())), preferred_element_type=f32
    ).astype(bf16)

    @pl.when(jnp.logical_not(has_below))
    def _():
        ext[0] = jnp.zeros(ext.shape[1:], bf16)

    @pl.when(jnp.logical_not(has_above))
    def _():
        ext[zc + 1] = jnp.zeros(ext.shape[1:], bf16)

    diagonals = 2 * (has_below.astype(i32) + has_above.astype(i32))
    pl.semaphore_wait(barrier, n_xy - 1 + n_gz - 1 + diagonals)

    def remote(src, dst, send, recv, target):
        return pltpu.make_async_remote_copy(
            src_ref=src,
            dst_ref=dst,
            send_sem=send,
            recv_sem=recv,
            device_id=target,
            device_id_type=MESH,
        )

    strip_copies = []
    for d, peer in enumerate(xy_peers):
        strip_copies += [
            remote(coords.at[xy], coords.at[xy], send_c.at[d], recv_c.at[d], {"xy": peer}),
            remote(q_all.at[xy], q_all.at[xy], send_q.at[d], recv_q.at[d], {"xy": peer}),
        ]
    for copy in strip_copies:
        copy.start()

    inner = pl.ds(1, zc)
    x_copies = [
        remote(ext.at[inner, 1], ext.at[inner, xc + 1], send_h.at[0], recv_h.at[0], {"xy": left}),
        remote(ext.at[inner, xc], ext.at[inner, 0], send_h.at[1], recv_h.at[1], {"xy": right}),
    ]

    def z_copies(first, own, ghost, target):
        strip = pl.ds(1, xc)
        return [
            remote(ext.at[own, strip], ext.at[ghost, strip], send_h.at[first], recv_h.at[first], {"gz": target}),
            remote(ext.at[own, 1], ext.at[ghost, xc + 1], send_h.at[first + 1], recv_h.at[first + 1], {"gz": target, "xy": left}),
            remote(ext.at[own, xc], ext.at[ghost, 0], send_h.at[first + 2], recv_h.at[first + 2], {"gz": target, "xy": right}),
        ]

    down = z_copies(2, 1, zc + 1, gz - 1)
    rise = z_copies(5, zc, 0, gz + 1)
    for copy in x_copies:
        copy.start()

    @pl.when(has_below)
    def _():
        for copy in down:
            copy.start()

    @pl.when(has_above)
    def _():
        for copy in rise:
            copy.start()

    def strip_phases(strip):
        at = jnp.transpose(coords[strip])
        turn = jnp.where(iota(i32, (1, 128), 1) < 64, 1, 0)
        step = 64
        for start in range(0, atoms, step):
            here = slice(start, start + step)
            at_x, at_y = at[here, 0:1], at[here, 1:2]
            lines = pl.ds(strip * atoms + start, step)
            quadrant, sine, cosine = reduced(at_x * cst[xy, 0:1, :128] + at_y * cst[xy, 1:2, :128])
            ph[lines, :128] = at_quadrant(quadrant + 1, sine, cosine).astype(bf16)
            ph[lines, 128:256] = at_quadrant(quadrant, sine, cosine).astype(bf16)
            quadrant, sine, cosine = reduced(at_x * cst[xy, 0:1, 256:] + at_y * cst[xy, 1:2, 256:])
            ph[lines, 256:] = at_quadrant(quadrant + turn, sine, cosine).astype(bf16)

    def strip_moments(strip):
        layer = coords[strip][2:3]
        charges = q_all[strip].astype(f32)
        weighted = jnp.concatenate(
            [jnp.where(layer == float(l), charges, 0.0) for l in range(layers)], axis=0
        ).astype(bf16)
        qw[strip] = weighted
        return dot(weighted, ph[pl.ds(strip * atoms, atoms), :])

    loads[7].wait()
    strip_phases(xy)
    total = strip_moments(xy)

    for load in loads[8:]:
        load.wait()
    d_all = dist[...]
    slot = iota(i32, (atoms, 1), 0) % slots
    entry = iota(i32, (atoms, entries), 1)
    usable = (entry < cols[:, 4:5].astype(i32)) & (near[...] != 4 * slots + slot)
    ratio = d_all * (1.0 / cutoff)
    envelope = 1.0 - ratio * ratio
    wgt[...] = jnp.where(usable, envelope * envelope, 0.0)
    basis_count, radial = radial_in.shape
    spread_shape = (entries, entries * basis_count)
    spread = (iota(i32, spread_shape, 1) // basis_count == iota(i32, spread_shape, 0)).astype(f32)
    spacing = jnp.dot(d_all, spread, precision=exact, preferred_element_type=f32)
    gap = spacing - centers[0:1, :]
    basis = jnp.exp(-(gap * gap)).astype(bf16)
    group = 128 // basis_count
    tall = jnp.concatenate([radial_in[...].astype(f32)] * group, axis=0)
    flat = jnp.concatenate([tall] * group, axis=1)
    diagonal = iota(i32, flat.shape, 0) // basis_count == iota(i32, flat.shape, 1) // radial
    hidden_in = jnp.where(diagonal, flat, 0.0).astype(bf16)
    for block in range(entries // group):
        for tile in range(flat.shape[1] // 256):
            pre = dot(basis[:, block * 128 : (block + 1) * 128], hidden_in[:, tile * 256 : (tile + 1) * 256])
            first = block * flat.shape[1] + tile * 256
            fh[:, first : first + 256] = silu(pre).astype(bf16)
    pack = 128 // radial
    tall = jnp.concatenate([radial_out[...].astype(f32)] * pack, axis=0)
    flat = jnp.concatenate([tall] * pack, axis=1)
    diagonal = iota(i32, flat.shape, 0) // radial == iota(i32, flat.shape, 1) // width
    hidden_out = jnp.where(diagonal, flat, 0.0).astype(bf16)

    for copy in strip_copies:
        copy.wait()

    def add_strip(d, total):
        strip = lax.rem(xy + d, n_xy)
        strip_phases(strip)
        return total + strip_moments(strip)

    total = lax.fori_loop(1, n_xy, add_strip, total)
    mine[...] = total

    def power(n):
        return cst[xy, 5 + n : 6 + n, :]

    def layer_moments(l):
        return mine[l * channels : (l + 1) * channels, :]

    tb[0] = sum(layer_moments(l) * power(layers - 1 - l) for l in range(layers))
    tb[1] = sum(layer_moments(l) * power(l) for l in range(layers))
    gz_copies = [
        remote(tb.at[jnp.where(peer > gz, 0, 1)], gz_buf.at[gz], send_g.at[d], recv_g.at[d], {"gz": peer})
        for d, peer in enumerate(gz_peers)
    ]
    for copy in gz_copies:
        copy.start()

    for copy in x_copies:
        copy.wait()

    @pl.when(has_below)
    def _():
        for copy in down:
            copy.wait_send()
        for copy in rise:
            copy.wait_recv()

    @pl.when(has_above)
    def _():
        for copy in rise:
            copy.wait_send()
        for copy in down:
            copy.wait_recv()

    half = 9 * slots // 2
    codes = iota(i32, (slots, half), 1)

    def edge_row(z):
        def one(x, carry):
            base = pl.multiple_of((z * xc + x) * slots, slots)
            region = ext[z : z + 3, pl.ds(x, 3)].reshape(9 * slots, width)
            region = jnp.concatenate([region[:half], region[half:]], axis=1)
            index = near[pl.ds(base, slots), :]
            upper = jnp.where(index >= half, 1, 0)
            folded = index - half * upper
            chosen = jnp.concatenate(
                [
                    jnp.where(folded[:, e : e + 1] == codes, 1.0, 0.0).astype(bf16)
                    for e in range(entries)
                ],
                axis=0,
            )
            gathered = dot(chosen, region)
            hid = fh[pl.ds(base, slots), :]
            both = jnp.concatenate(
                [hid[:, p * 128 : (p + 1) * 128] for p in range(hid.shape[1] // 128)], axis=0
            )
            filters = dot(both, hidden_out)
            weight = wgt[pl.ds(base, slots), :]
            acc = jnp.zeros((slots, width), f32)
            for e in range(entries):
                row, col = (e // pack) * slots, (e % pack) * width
                filtered = weight[:, e : e + 1] * filters[row : row + slots, col : col + width]
                pair = gathered[e * slots : (e + 1) * slots]
                rows_of = jnp.where(upper[:, e : e + 1] == 1, pair[:, width:], pair[:, :width])
                acc = acc + filtered * rows_of
            agg[pl.ds(base, slots), :] = acc.astype(bf16)
            return carry

        lax.fori_loop(0, xc, one, 0)

    for z in range(zc // 2):
        edge_row(z)

    for copy in gz_copies:
        copy.wait()
    span = power(layers)
    none = jnp.zeros(tb.shape[1:], f32)
    from_below = lax.fori_loop(0, gz, lambda t, s: s * span + gz_buf[t], none)
    from_above = lax.fori_loop(0, n_gz - 1 - gz, lambda t, s: s * span + gz_buf[n_gz - 1 - t], none)
    for l in range(layers):
        value = power(l + 1) * from_below + power(layers - l) * from_above
        for m in range(layers):
            value = value + power(abs(l - m)) * layer_moments(m)
        value = value * cst[xy, 2:3, :]
        swapped = jnp.concatenate(
            [value[:, 128:256], value[:, :128], value[:, 320:], value[:, 256:320]], axis=1
        )
        lines = (value, cst[xy, 3:4, :] * swapped, cst[xy, 4:5, :] * swapped)
        for r, line in enumerate(lines):
            top = r * pairs + l * channels
            panel[top : top + channels, :] = line.astype(bf16)

    def strip_sums(strip):
        evaluated = lax.dot_general(
            panel[...],
            ph[pl.ds(strip * atoms, atoms), :],
            (((1,), (1,)), ((), ())),
            preferred_element_type=f32,
        )
        charges = qw[strip].astype(f32)
        lines = [
            jnp.sum(evaluated[r * pairs : (r + 1) * pairs] * charges, axis=0, keepdims=True)
            for r in range(3)
        ]
        return jnp.concatenate(lines + [jnp.zeros((5, atoms), f32)], axis=0)

    part_copies = []
    for d, peer in enumerate(xy_peers):
        part[d] = strip_sums(peer)
        copy = remote(part.at[d], part_buf.at[d], send_p.at[d], recv_p.at[d], {"xy": peer})
        copy.start()
        part_copies.append(copy)
    own_rows[...] = strip_sums(xy)

    for z in range(zc // 2, zc):
        edge_row(z)

    updated = silu(dot(agg[...], update_in[...])).astype(bf16)
    renewed = ext[1 : zc + 1, 1 : xc + 1].reshape(atoms, width).astype(f32) + dot(updated, update_out[...])
    out_feat[...] = renewed.astype(bf16)
    readout = jnp.broadcast_to(energy_w[0:1, :].astype(f32), (8, width))
    energy = lax.dot_general(
        readout, renewed, (((1,), (1,)), ((), ())), precision=exact, preferred_element_type=f32
    )

    for copy in part_copies:
        copy.wait()
    sums = own_rows[...]
    for d in range(n_xy - 1):
        sums = sums + part_buf[d]
    finals = (energy[0:1] + 0.5 * sums[0:1], -sums[1:2], -sums[2:3])
    spread_out = jnp.concatenate([jnp.where(own_cell, line, 0.0) for line in finals], axis=0)
    folded = lax.dot_general(
        spread_out, unfold, (((1,), (1,)), ((), ())), precision=exact, preferred_element_type=f32
    )
    out_energy[...] = folded[:cells]
    out_forces[...] = folded[cells:]


def shards(
    n_xy,
    n_gz,
    features,
    species,
    sublayer,
    offsets,
    neighbours,
    neighbour_count,
    distances,
    species_table,
    charge_weight,
    radial_in,
    radial_out,
    update_in,
    update_out,
    energy_weight,
):
    f32, bf16 = jnp.float32, jnp.bfloat16
    zc, xc, slots, width = features.shape
    entries = neighbours.shape[3]
    channels = charge_weight.shape[1]
    cells = zc * xc
    atoms = cells * slots
    layers = 2 * zc
    pairs = layers * channels
    basis_count, radial = radial_in.shape
    cst = wave_constants(cell_width * (xc * n_xy), layers, n_xy)
    mids = np.float32(cutoff) * np.arange(basis_count).astype(np.float32) / np.float32(basis_count - 1)
    centers = np.tile(mids, (8, entries)).astype(np.float32)
    sizes = (zc, xc, slots, entries, channels, n_xy, n_gz)
    dma = pltpu.SemaphoreType.DMA
    vmem = pl.BlockSpec(memory_space=pltpu.VMEM)
    operands = (
        species.reshape(cells, slots),
        sublayer.reshape(cells, slots),
        neighbour_count.reshape(cells, slots),
        offsets.reshape(2 * cells, slots),
        features.reshape(atoms, width),
        species_table,
        charge_weight.T,
        jnp.asarray(cst),
        distances.reshape(atoms, entries),
        neighbours.reshape(atoms, entries),
        jnp.asarray(centers),
        radial_in,
        radial_out,
        update_in,
        update_out,
        energy_weight.reshape(1, width),
    )
    hbm = pl.BlockSpec(memory_space=pltpu.HBM)
    shapes = (
        jax.ShapeDtypeStruct((atoms, width), bf16),
        jax.ShapeDtypeStruct((cells, slots), f32),
        jax.ShapeDtypeStruct((2 * cells, slots), f32),
    )
    results = pl.pallas_call(
        functools.partial(kernel, sizes),
        out_shape=shapes,
        in_specs=[hbm] * INPUTS,
        out_specs=(vmem, vmem, vmem),
        scratch_shapes=[pltpu.VMEM(a.shape, a.dtype) for a in operands]
        + [
            dma((INPUTS,)),
            pltpu.VMEM((zc + 2, xc + 2, slots, width), bf16),
            pltpu.VMEM((n_xy * atoms, LANES), bf16),
            pltpu.VMEM((atoms, entries * radial), bf16),
            pltpu.VMEM((atoms, entries), f32),
            pltpu.VMEM((atoms, width), bf16),
            pltpu.VMEM((8, atoms), f32),
            pltpu.VMEM((n_xy, 8, atoms), f32),
            pltpu.VMEM((n_xy, channels, atoms), bf16),
            pltpu.VMEM((n_xy, pairs, atoms), bf16),
            pltpu.VMEM((2, channels, LANES), f32),
            pltpu.VMEM((n_gz, channels, LANES), f32),
            pltpu.VMEM((pairs, LANES), f32),
            pltpu.VMEM((3 * pairs, LANES), bf16),
            pltpu.VMEM((n_xy - 1, 8, atoms), f32),
            pltpu.VMEM((n_xy - 1, 8, atoms), f32),
            dma((8,)),
            dma((8,)),
            dma((n_xy - 1,)),
            dma((n_xy - 1,)),
            dma((n_xy - 1,)),
            dma((n_xy - 1,)),
            dma((n_gz - 1,)),
            dma((n_gz - 1,)),
            dma((n_xy - 1,)),
            dma((n_xy - 1,)),
        ],
        compiler_params=pltpu.CompilerParams(
            collective_id=0, has_side_effects=True, vmem_limit_bytes=60 * 1024 * 1024
        ),
        cost_estimate=pl.CostEstimate(flops=2_000_000_000, bytes_accessed=2_000_000, transcendentals=2_000_000),
    )(*operands)
    out_feat, energy, forces = pl.pallas_call(
        writer,
        out_shape=shapes,
        in_specs=[vmem] * 3,
        out_specs=(hbm, hbm, hbm),
        scratch_shapes=[dma((3,))],
    )(*results)
    return (
        out_feat.reshape(features.shape),
        energy.reshape(species.shape),
        forces.reshape((2,) + species.shape),
    )


def solution(mesh):
    atom = P(("groups", "gz"), "xy", None)
    atom_wide = P(("groups", "gz"), "xy", None, None)
    pair = P(None, ("groups", "gz"), "xy", None)
    in_specs = (atom_wide, atom, atom, pair, atom_wide, atom, atom_wide) + (P(),) * 7
    body = functools.partial(shards, mesh.shape["xy"], mesh.shape["gz"])
    return jax.shard_map(
        body, mesh=mesh, in_specs=in_specs, out_specs=(atom_wide, atom, pair), check_vma=False
    )
```

```python
import functools
import math

import jax
import jax.numpy as jnp
import numpy as np
from jax import lax
from jax.experimental import pallas as pl
from jax.experimental.pallas import tpu as pltpu
from jax.sharding import PartitionSpec as P

KX = 128
KY = 8
MESH = pl.DeviceIdType.MESH

cell_width = 11.0
layer_depth = 5.5
screening = 0.025
smearing = 1.0
coupling = 0.25
cutoff = 8.0

BLOCKS = (4, 0, 5, 6, 7)
LANES = 384


def wave_constants(width_x, layers, n_xy):
    f32 = np.float32
    per = KX // n_xy

    def factors(index_x, index_y, count):
        wave_x = f32(2.0 * math.pi / width_x) * (index_x - KX // 2).astype(f32)
        wave_y = f32(2.0 * math.pi / cell_width) * (index_y - KY // 2).astype(f32)
        square = wave_x * wave_x + wave_y * wave_y
        screened = np.sqrt(square + f32(screening * screening))
        weight = f32(coupling * (2.0 * math.pi / (width_x * cell_width))) * np.exp(
            f32(-0.5 * smearing * smearing) * square
        )
        quarter_x = (4.0 / width_x * (index_x - KX // 2)).astype(f32)
        quarter_y = (4.0 / cell_width * (index_y - KY // 2)).astype(f32)
        return wave_x, wave_y, weight / screened * count, screened, quarter_x, quarter_y

    strips = []
    for strip in range(n_xy):
        own = np.arange(strip * per, (strip + 1) * per)
        index_x = np.tile(own, len(BLOCKS) - 1)
        index_y = np.repeat(np.array(BLOCKS[1:]), per)
        count = np.where((index_y > KY // 2) & (index_x > 0), 2.0, 1.0).astype(f32)
        part_a = factors(index_x, index_y, count)
        index_x, index_y = own.copy(), np.full(per, KY // 2)
        count = np.where((own > 0) & (own < KX // 2), 2.0, 1.0).astype(f32)
        count[own > KX // 2] = 0.0
        for spare, j in enumerate((1, 2, 3)):
            place = KX // 2 + 1 + spare
            count[own == place] = 1.0
            index_y[own == place] = j
            index_x[own == place] = 0
        part_b = factors(index_x, index_y, count)
        lanes = []
        for one, two in zip(part_a, part_b):
            one = np.pad(one, (0, 128 - one.size))
            two = np.pad(two, (0, 32 - two.size))
            lanes.append(np.concatenate([one, one, two, two, two, two]))
        wave_x, wave_y, weight, screened, *quarters = lanes
        sign = np.repeat(np.array([1, -1, 1, -1, 1, -1], f32), [128, 128, 32, 32, 32, 32])
        powers = [np.exp(-screened * f32(layer_depth) * f32(n)) for n in range(layers + 1)]
        rows = [*quarters, weight, sign * wave_x, sign * wave_y] + powers
        rows += [np.zeros(LANES, f32)] * (-len(rows) % 8)
        strips.append(np.stack(rows))
    return np.stack(strips).astype(f32)


def reduced(quarters):
    whole = (quarters + 12582912.0) - 12582912.0
    rest = quarters - whole
    square = rest * rest
    q = math.pi / 2.0
    sine = rest * (
        (((-1.9515295891e-4 * q**7) * square + 8.3321608736e-3 * q**5) * square - 1.6666654611e-1 * q**3)
        * square
        + q
    )
    cosine = (
        (((2.443315711809948e-5 * q**8) * square - 1.388731625493765e-3 * q**6) * square
         + 4.166664568298827e-2 * q**4) * square - 0.5 * q**2
    ) * square + 1.0
    return whole.astype(jnp.int32), sine, cosine


def at_quadrant(quadrant, sine, cosine):
    value = jnp.where((quadrant & 1) == 1, cosine, sine)
    return jnp.where((quadrant & 2) == 2, -value, value)


def silu(value):
    half = 0.5 * value
    return half + half * jnp.tanh(half)


def dot(a, b):
    return jnp.dot(a, b, preferred_element_type=jnp.float32)


INPUTS = 16


def writer(feat_in, energy_in, forces_in, feat_out, energy_out, forces_out, sems):
    pairs = ((feat_in, feat_out), (energy_in, energy_out), (forces_in, forces_out))
    copies = [pltpu.make_async_copy(a, b, sems.at[i]) for i, (a, b) in enumerate(pairs)]
    for copy in copies:
        copy.start()
    for copy in copies:
        copy.wait()


def kernel(sizes, *refs):
    in_hbm, refs = refs[:INPUTS], refs[INPUTS:]
    (out_feat, out_energy, out_forces), refs = refs[:3], refs[3:]
    held, refs = refs[:INPUTS], refs[INPUTS:]
    (
        load_sem,
        ext,
        ph,
        fh,
        wgt,
        agg,
        own_rows,
        coords,
        q_all,
        qw,
        tb,
        gz_buf,
        mine,
        panel,
        part,
        part_buf,
        send_h,
        recv_h,
        send_c,
        recv_c,
        send_q,
        recv_q,
        send_g,
        recv_g,
        send_p,
        recv_p,
    ) = refs
    (
        species,
        sublayer,
        counts,
        offsets,
        feat,
        table,
        charge_w,
        cst,
        dist,
        near,
        centers,
        radial_in,
        radial_out,
        update_in,
        update_out,
        energy_w,
    ) = held
    loads = [
        pltpu.make_async_copy(a, b, load_sem.at[i]) for i, (a, b) in enumerate(zip(in_hbm, held))
    ]
    for load in loads:
        load.start()
    zc, xc, slots, entries, channels, n_xy, n_gz = sizes
    cells = zc * xc
    atoms = cells * slots
    layers = 2 * zc
    pairs = layers * channels
    f32, bf16, i32 = jnp.float32, jnp.bfloat16, jnp.int32
    exact = lax.Precision.HIGHEST
    iota = lax.broadcasted_iota
    width = feat.shape[1]
    gz = lax.axis_index("gz")
    xy = lax.axis_index("xy")
    left, right = lax.rem(xy + n_xy - 1, n_xy), lax.rem(xy + 1, n_xy)
    xy_peers = [lax.rem(xy + d, n_xy) for d in range(1, n_xy)]
    gz_peers = [lax.rem(gz + d, n_gz) for d in range(1, n_gz)]
    has_below = gz > 0
    has_above = gz < n_gz - 1

    barrier = pltpu.get_barrier_semaphore()
    for peer in xy_peers:
        pl.semaphore_signal(barrier, inc=1, device_id={"xy": peer}, device_id_type=MESH)
    for peer in gz_peers:
        pl.semaphore_signal(barrier, inc=1, device_id={"gz": peer}, device_id_type=MESH)
    for present, step in ((has_below, -1), (has_above, 1)):

        @pl.when(present)
        def _():
            for side in (left, right):
                pl.semaphore_signal(
                    barrier, inc=1, device_id={"gz": gz + step, "xy": side}, device_id_type=MESH
                )

    for load in loads[:4]:
        load.wait()
    unfold = (iota(i32, (slots, atoms), 1) % slots == iota(i32, (slots, atoms), 0)).astype(f32)
    own_cell = iota(i32, (cells, atoms), 1) // slots == iota(i32, (cells, atoms), 0)
    stacked = jnp.concatenate(
        [species[...].astype(f32), sublayer[...].astype(f32), counts[...].astype(f32), offsets[...]],
        axis=0,
    )
    wide = jnp.dot(stacked, unfold, precision=exact, preferred_element_type=f32)
    kind_row, sub_row, count_row, x_row, y_row = [
        jnp.sum(jnp.where(own_cell, wide[i * cells : (i + 1) * cells], 0.0), axis=0, keepdims=True)
        for i in range(5)
    ]
    atom_cell = iota(i32, (1, atoms), 1) // slots
    x_row = cell_width * (xy * xc + atom_cell % xc).astype(f32) + x_row
    layer_row = sub_row + (2 * (atom_cell // xc)).astype(f32)
    blank = jnp.zeros((3, atoms), f32)
    rows = jnp.concatenate([x_row, y_row, layer_row, kind_row, count_row, blank], axis=0)
    coords[xy] = rows
    cols = jnp.transpose(rows)

    for load in loads[4:7]:
        load.wait()
    kinds = table.shape[0]
    onehot = cols[:, 3:4] == iota(i32, (atoms, kinds), 1).astype(f32)
    hidden = (feat[...].astype(f32) + dot(onehot.astype(f32).astype(bf16), table[...])).astype(bf16)
    ext[1 : zc + 1, 1 : xc + 1] = hidden.reshape(zc, xc, slots, width)
    q_all[xy] = lax.dot_general(
        charge_w[...], hidden, (((1,), (1,)), ((), ())), preferred_element_type=f32
    ).astype(bf16)

    @pl.when(jnp.logical_not(has_below))
    def _():
        ext[0] = jnp.zeros(ext.shape[1:], bf16)

    @pl.when(jnp.logical_not(has_above))
    def _():
        ext[zc + 1] = jnp.zeros(ext.shape[1:], bf16)

    diagonals = 2 * (has_below.astype(i32) + has_above.astype(i32))
    pl.semaphore_wait(barrier, n_xy - 1 + n_gz - 1 + diagonals)

    def remote(src, dst, send, recv, target):
        return pltpu.make_async_remote_copy(
            src_ref=src,
            dst_ref=dst,
            send_sem=send,
            recv_sem=recv,
            device_id=target,
            device_id_type=MESH,
        )

    strip_copies = []
    for d, peer in enumerate(xy_peers):
        strip_copies += [
            remote(coords.at[xy], coords.at[xy], send_c.at[d], recv_c.at[d], {"xy": peer}),
            remote(q_all.at[xy], q_all.at[xy], send_q.at[d], recv_q.at[d], {"xy": peer}),
        ]
    for copy in strip_copies:
        copy.start()

    inner = pl.ds(1, zc)
    x_copies = [
        remote(ext.at[inner, 1], ext.at[inner, xc + 1], send_h.at[0], recv_h.at[0], {"xy": left}),
        remote(ext.at[inner, xc], ext.at[inner, 0], send_h.at[1], recv_h.at[1], {"xy": right}),
    ]

    def z_copies(first, own, ghost, target):
        strip = pl.ds(1, xc)
        return [
            remote(ext.at[own, strip], ext.at[ghost, strip], send_h.at[first], recv_h.at[first], {"gz": target}),
            remote(ext.at[own, 1], ext.at[ghost, xc + 1], send_h.at[first + 1], recv_h.at[first + 1], {"gz": target, "xy": left}),
            remote(ext.at[own, xc], ext.at[ghost, 0], send_h.at[first + 2], recv_h.at[first + 2], {"gz": target, "xy": right}),
        ]

    down = z_copies(2, 1, zc + 1, gz - 1)
    rise = z_copies(5, zc, 0, gz + 1)
    for copy in x_copies:
        copy.start()

    @pl.when(has_below)
    def _():
        for copy in down:
            copy.start()

    @pl.when(has_above)
    def _():
        for copy in rise:
            copy.start()

    def strip_phases(strip):
        at = jnp.transpose(coords[strip])
        lane = iota(i32, (1, 128), 1)
        turn = jnp.where(lane % 64 < 32, 1, 0)
        first = lane < 64
        step = 64
        for start in range(0, atoms // 2, step):
            value = []
            for part in range(2):
                row = start + part * (atoms // 2)
                at_x, at_y = at[row : row + step, 0:1], at[row : row + step, 1:2]
                lines = pl.ds(strip * atoms + row, step)
                quadrant, sine, cosine = reduced(at_x * cst[xy, 0:1, :128] + at_y * cst[xy, 1:2, :128])
                ph[lines, :128] = at_quadrant(quadrant + 1, sine, cosine).astype(bf16)
                ph[lines, 128:256] = at_quadrant(quadrant, sine, cosine).astype(bf16)
                value.append(at_x * cst[xy, 0:1, 256:] + at_y * cst[xy, 1:2, 256:])
            quadrant, sine, cosine = reduced(jnp.where(first, value[0], value[1]))
            both = at_quadrant(quadrant + turn, sine, cosine)
            for part in range(2):
                lines = pl.ds(strip * atoms + start + part * (atoms // 2), step)
                ph[lines, 256:] = jnp.where(first == (part == 0), both, 0.0).astype(bf16)

    def strip_moments(strip):
        layer = coords[strip][2:3]
        charges = q_all[strip].astype(f32)
        weighted = jnp.concatenate(
            [jnp.where(layer == float(l), charges, 0.0) for l in range(layers)], axis=0
        ).astype(bf16)
        qw[strip] = weighted
        return dot(weighted, ph[pl.ds(strip * atoms, atoms), :])

    loads[7].wait()
    strip_phases(xy)
    total = strip_moments(xy)

    for load in loads[8:]:
        load.wait()
    d_all = dist[...]
    slot = iota(i32, (atoms, 1), 0) % slots
    entry = iota(i32, (atoms, entries), 1)
    usable = (entry < cols[:, 4:5].astype(i32)) & (near[...] != 4 * slots + slot)
    ratio = d_all * (1.0 / cutoff)
    envelope = 1.0 - ratio * ratio
    wgt[...] = jnp.where(usable, envelope * envelope, 0.0)
    basis_count, radial = radial_in.shape
    spread_shape = (entries, entries * basis_count)
    spread = (iota(i32, spread_shape, 1) // basis_count == iota(i32, spread_shape, 0)).astype(f32)
    spacing = jnp.dot(d_all, spread, precision=exact, preferred_element_type=f32)
    gap = spacing - centers[0:1, :]
    basis = jnp.exp(-(gap * gap)).astype(bf16)
    group = 128 // basis_count
    tall = jnp.concatenate([radial_in[...].astype(f32)] * group, axis=0)
    flat = jnp.concatenate([tall] * group, axis=1)
    diagonal = iota(i32, flat.shape, 0) // basis_count == iota(i32, flat.shape, 1) // radial
    hidden_in = jnp.where(diagonal, flat, 0.0).astype(bf16)
    for block in range(entries // group):
        for tile in range(flat.shape[1] // 256):
            pre = dot(basis[:, block * 128 : (block + 1) * 128], hidden_in[:, tile * 256 : (tile + 1) * 256])
            first = block * flat.shape[1] + tile * 256
            fh[:, first : first + 256] = silu(pre).astype(bf16)
    pack = 128 // radial
    tall = jnp.concatenate([radial_out[...].astype(f32)] * pack, axis=0)
    flat = jnp.concatenate([tall] * pack, axis=1)
    diagonal = iota(i32, flat.shape, 0) // radial == iota(i32, flat.shape, 1) // width
    hidden_out = jnp.where(diagonal, flat, 0.0).astype(bf16)

    for copy in strip_copies:
        copy.wait()

    def add_strip(d, total):
        strip = lax.rem(xy + d, n_xy)
        strip_phases(strip)
        return total + strip_moments(strip)

    total = lax.fori_loop(1, n_xy, add_strip, total)
    spare = total[:, 256:]
    mine[:, :256] = total[:, :256]
    mine[:, 256:] = spare + jnp.concatenate([spare[:, 64:], spare[:, :64]], axis=1)

    def power(n):
        return cst[xy, 5 + n : 6 + n, :]

    def layer_moments(l):
        return mine[l * channels : (l + 1) * channels, :]

    tb[0] = sum(layer_moments(l) * power(layers - 1 - l) for l in range(layers))
    tb[1] = sum(layer_moments(l) * power(l) for l in range(layers))
    gz_copies = [
        remote(tb.at[jnp.where(peer > gz, 0, 1)], gz_buf.at[gz], send_g.at[d], recv_g.at[d], {"gz": peer})
        for d, peer in enumerate(gz_peers)
    ]
    for copy in gz_copies:
        copy.start()

    for copy in x_copies:
        copy.wait()

    @pl.when(has_below)
    def _():
        for copy in down:
            copy.wait_send()
        for copy in rise:
            copy.wait_recv()

    @pl.when(has_above)
    def _():
        for copy in rise:
            copy.wait_send()
        for copy in down:
            copy.wait_recv()

    half = 9 * slots // 2
    codes = iota(i32, (slots, half), 1).astype(f32).astype(bf16)
    hit, miss = jnp.ones(codes.shape, bf16), jnp.zeros(codes.shape, bf16)

    def edge_row(z):
        def one(x, carry):
            base = pl.multiple_of((z * xc + x) * slots, slots)
            region = ext[z : z + 3, pl.ds(x, 3)].reshape(9 * slots, width)
            region = jnp.concatenate([region[:half], region[half:]], axis=1)
            index = near[pl.ds(base, slots), :]
            upper = index >= half
            folded = jnp.where(upper, index - half, index).astype(f32).astype(bf16)
            weight = wgt[pl.ds(base, slots), :]
            signed = jnp.where(upper, -weight, weight)
            chosen = jnp.concatenate(
                [jnp.where(folded[:, e : e + 1] == codes, hit, miss) for e in range(entries)], axis=0
            )
            gathered = dot(chosen, region)
            hid = fh[pl.ds(base, slots), :]
            both = jnp.concatenate(
                [hid[:, p * 128 : (p + 1) * 128] for p in range(hid.shape[1] // 128)], axis=0
            )
            filters = dot(both, hidden_out)
            acc = jnp.zeros((slots, width), f32)
            for e in range(entries):
                row, col = (e // pack) * slots, (e % pack) * width
                mark = jnp.broadcast_to(signed[:, e : e + 1], (slots, width))
                filtered = jnp.abs(mark) * filters[row : row + slots, col : col + width]
                pair = gathered[e * slots : (e + 1) * slots]
                rows_of = jnp.where(mark < 0.0, pair[:, width:], pair[:, :width])
                acc = acc + filtered * rows_of
            agg[pl.ds(base, slots), :] = acc.astype(bf16)
            return carry

        lax.fori_loop(0, xc, one, 0, unroll=2)

    for z in range(zc // 2):
        edge_row(z)

    for copy in gz_copies:
        copy.wait()
    span = power(layers)
    none = jnp.zeros(tb.shape[1:], f32)
    from_below = lax.fori_loop(0, gz, lambda t, s: s * span + gz_buf[t], none)
    from_above = lax.fori_loop(0, n_gz - 1 - gz, lambda t, s: s * span + gz_buf[n_gz - 1 - t], none)
    for l in range(layers):
        value = power(l + 1) * from_below + power(layers - l) * from_above
        for m in range(layers):
            value = value + power(abs(l - m)) * layer_moments(m)
        value = value * cst[xy, 2:3, :]
        swapped = jnp.concatenate(
            [value[:, 128:256], value[:, :128]]
            + [value[:, 256 + 32 * n : 288 + 32 * n] for n in (1, 0, 3, 2)],
            axis=1,
        )
        lines = (value, cst[xy, 3:4, :] * swapped, cst[xy, 4:5, :] * swapped)
        for r, line in enumerate(lines):
            top = r * pairs + l * channels
            panel[top : top + channels, :] = line.astype(bf16)

    def strip_sums(strip):
        evaluated = lax.dot_general(
            panel[...],
            ph[pl.ds(strip * atoms, atoms), :],
            (((1,), (1,)), ((), ())),
            preferred_element_type=f32,
        )
        charges = qw[strip].astype(f32)
        lines = [
            jnp.sum(evaluated[r * pairs : (r + 1) * pairs] * charges, axis=0, keepdims=True)
            for r in range(3)
        ]
        return jnp.concatenate(lines + [jnp.zeros((5, atoms), f32)], axis=0)

    part_copies = []
    for d, peer in enumerate(xy_peers):
        part[d] = strip_sums(peer)
        copy = remote(part.at[d], part_buf.at[d], send_p.at[d], recv_p.at[d], {"xy": peer})
        copy.start()
        part_copies.append(copy)
    own_rows[...] = strip_sums(xy)

    for z in range(zc // 2, zc):
        edge_row(z)

    updated = silu(dot(agg[...], update_in[...])).astype(bf16)
    renewed = ext[1 : zc + 1, 1 : xc + 1].reshape(atoms, width).astype(f32) + dot(updated, update_out[...])
    out_feat[...] = renewed.astype(bf16)
    readout = jnp.broadcast_to(energy_w[0:1, :].astype(f32), (8, width))
    energy = lax.dot_general(
        readout, renewed, (((1,), (1,)), ((), ())), precision=exact, preferred_element_type=f32
    )

    for copy in part_copies:
        copy.wait()
    sums = own_rows[...]
    for d in range(n_xy - 1):
        sums = sums + part_buf[d]
    finals = (energy[0:1] + 0.5 * sums[0:1], -sums[1:2], -sums[2:3])
    spread_out = jnp.concatenate([jnp.where(own_cell, line, 0.0) for line in finals], axis=0)
    folded = lax.dot_general(
        spread_out, unfold, (((1,), (1,)), ((), ())), precision=exact, preferred_element_type=f32
    )
    out_energy[...] = folded[:cells]
    out_forces[...] = folded[cells:]


def shards(
    n_xy,
    n_gz,
    features,
    species,
    sublayer,
    offsets,
    neighbours,
    neighbour_count,
    distances,
    species_table,
    charge_weight,
    radial_in,
    radial_out,
    update_in,
    update_out,
    energy_weight,
):
    f32, bf16 = jnp.float32, jnp.bfloat16
    zc, xc, slots, width = features.shape
    entries = neighbours.shape[3]
    channels = charge_weight.shape[1]
    cells = zc * xc
    atoms = cells * slots
    layers = 2 * zc
    pairs = layers * channels
    basis_count, radial = radial_in.shape
    cst = wave_constants(cell_width * (xc * n_xy), layers, n_xy)
    mids = np.float32(cutoff) * np.arange(basis_count).astype(np.float32) / np.float32(basis_count - 1)
    centers = np.tile(mids, (8, entries)).astype(np.float32)
    sizes = (zc, xc, slots, entries, channels, n_xy, n_gz)
    dma = pltpu.SemaphoreType.DMA
    vmem = pl.BlockSpec(memory_space=pltpu.VMEM)
    operands = (
        species.reshape(cells, slots),
        sublayer.reshape(cells, slots),
        neighbour_count.reshape(cells, slots),
        offsets.reshape(2 * cells, slots),
        features.reshape(atoms, width),
        species_table,
        charge_weight.T,
        jnp.asarray(cst),
        distances.reshape(atoms, entries),
        neighbours.reshape(atoms, entries),
        jnp.asarray(centers),
        radial_in,
        radial_out,
        update_in,
        update_out,
        energy_weight.reshape(1, width),
    )
    hbm = pl.BlockSpec(memory_space=pltpu.HBM)
    shapes = (
        jax.ShapeDtypeStruct((atoms, width), bf16),
        jax.ShapeDtypeStruct((cells, slots), f32),
        jax.ShapeDtypeStruct((2 * cells, slots), f32),
    )
    results = pl.pallas_call(
        functools.partial(kernel, sizes),
        out_shape=shapes,
        in_specs=[hbm] * INPUTS,
        out_specs=(vmem, vmem, vmem),
        scratch_shapes=[pltpu.VMEM(a.shape, a.dtype) for a in operands]
        + [
            dma((INPUTS,)),
            pltpu.VMEM((zc + 2, xc + 2, slots, width), bf16),
            pltpu.VMEM((n_xy * atoms, LANES), bf16),
            pltpu.VMEM((atoms, entries * radial), bf16),
            pltpu.VMEM((atoms, entries), f32),
            pltpu.VMEM((atoms, width), bf16),
            pltpu.VMEM((8, atoms), f32),
            pltpu.VMEM((n_xy, 8, atoms), f32),
            pltpu.VMEM((n_xy, channels, atoms), bf16),
            pltpu.VMEM((n_xy, pairs, atoms), bf16),
            pltpu.VMEM((2, channels, LANES), f32),
            pltpu.VMEM((n_gz, channels, LANES), f32),
            pltpu.VMEM((pairs, LANES), f32),
            pltpu.VMEM((3 * pairs, LANES), bf16),
            pltpu.VMEM((n_xy - 1, 8, atoms), f32),
            pltpu.VMEM((n_xy - 1, 8, atoms), f32),
            dma((8,)),
            dma((8,)),
            dma((n_xy - 1,)),
            dma((n_xy - 1,)),
            dma((n_xy - 1,)),
            dma((n_xy - 1,)),
            dma((n_gz - 1,)),
            dma((n_gz - 1,)),
            dma((n_xy - 1,)),
            dma((n_xy - 1,)),
        ],
        compiler_params=pltpu.CompilerParams(
            collective_id=0, has_side_effects=True, vmem_limit_bytes=60 * 1024 * 1024
        ),
        cost_estimate=pl.CostEstimate(flops=2_000_000_000, bytes_accessed=2_000_000, transcendentals=2_000_000),
    )(*operands)
    out_feat, energy, forces = pl.pallas_call(
        writer,
        out_shape=shapes,
        in_specs=[vmem] * 3,
        out_specs=(hbm, hbm, hbm),
        scratch_shapes=[dma((3,))],
    )(*results)
    return (
        out_feat.reshape(features.shape),
        energy.reshape(species.shape),
        forces.reshape((2,) + species.shape),
    )


def solution(mesh):
    atom = P(("groups", "gz"), "xy", None)
    atom_wide = P(("groups", "gz"), "xy", None, None)
    pair = P(None, ("groups", "gz"), "xy", None)
    in_specs = (atom_wide, atom, atom, pair, atom_wide, atom, atom_wide) + (P(),) * 7
    body = functools.partial(shards, mesh.shape["xy"], mesh.shape["gz"])
    return jax.shard_map(
        body, mesh=mesh, in_specs=in_specs, out_specs=(atom_wide, atom, pair), check_vma=False
    )
```

```python
import functools
import math

import jax
import jax.numpy as jnp
import numpy as np
from jax import lax
from jax.experimental import pallas as pl
from jax.experimental.pallas import tpu as pltpu
from jax.sharding import PartitionSpec as P

KX = 128
KY = 8
MESH = pl.DeviceIdType.MESH

cell_width = 11.0
layer_depth = 5.5
screening = 0.025
smearing = 1.0
coupling = 0.25
cutoff = 8.0

BLOCKS = (4, 0, 5, 6, 7)
LANES = 384


def wave_constants(width_x, layers, n_xy):
    f32 = np.float32
    per = KX // n_xy

    def factors(index_x, index_y, count):
        wave_x = f32(2.0 * math.pi / width_x) * (index_x - KX // 2).astype(f32)
        wave_y = f32(2.0 * math.pi / cell_width) * (index_y - KY // 2).astype(f32)
        square = wave_x * wave_x + wave_y * wave_y
        screened = np.sqrt(square + f32(screening * screening))
        weight = f32(coupling * (2.0 * math.pi / (width_x * cell_width))) * np.exp(
            f32(-0.5 * smearing * smearing) * square
        )
        quarter_x = (4.0 / width_x * (index_x - KX // 2)).astype(f32)
        quarter_y = (4.0 / cell_width * (index_y - KY // 2)).astype(f32)
        return wave_x, wave_y, weight / screened * count, screened, quarter_x, quarter_y

    strips = []
    for strip in range(n_xy):
        own = np.arange(strip * per, (strip + 1) * per)
        index_x = np.tile(own, len(BLOCKS) - 1)
        index_y = np.repeat(np.array(BLOCKS[1:]), per)
        count = np.where((index_y > KY // 2) & (index_x > 0), 2.0, 1.0).astype(f32)
        part_a = factors(index_x, index_y, count)
        index_x, index_y = own.copy(), np.full(per, KY // 2)
        count = np.where((own > 0) & (own < KX // 2), 2.0, 1.0).astype(f32)
        count[own > KX // 2] = 0.0
        for spare, j in enumerate((1, 2, 3)):
            place = KX // 2 + 1 + spare
            count[own == place] = 1.0
            index_y[own == place] = j
            index_x[own == place] = 0
        part_b = factors(index_x, index_y, count)
        lanes = []
        for one, two in zip(part_a, part_b):
            one = np.pad(one, (0, 128 - one.size))
            two = np.pad(two, (0, 32 - two.size))
            lanes.append(np.concatenate([one, one, two, two, two, two]))
        wave_x, wave_y, weight, screened, *quarters = lanes
        sign = np.repeat(np.array([1, -1, 1, -1, 1, -1], f32), [128, 128, 32, 32, 32, 32])
        powers = [np.exp(-screened * f32(layer_depth) * f32(n)) for n in range(layers + 1)]
        rows = [*quarters, weight, sign * wave_x, sign * wave_y] + powers
        rows += [np.zeros(LANES, f32)] * (-len(rows) % 8)
        strips.append(np.stack(rows))
    return np.stack(strips).astype(f32)


def reduced(quarters):
    whole = (quarters + 12582912.0) - 12582912.0
    rest = quarters - whole
    square = rest * rest
    q = math.pi / 2.0
    sine = rest * (
        (((-1.9515295891e-4 * q**7) * square + 8.3321608736e-3 * q**5) * square - 1.6666654611e-1 * q**3)
        * square
        + q
    )
    cosine = (
        (((2.443315711809948e-5 * q**8) * square - 1.388731625493765e-3 * q**6) * square
         + 4.166664568298827e-2 * q**4) * square - 0.5 * q**2
    ) * square + 1.0
    return whole.astype(jnp.int32), sine, cosine


def at_quadrant(quadrant, sine, cosine):
    value = jnp.where((quadrant & 1) == 1, cosine, sine)
    return jnp.where((quadrant & 2) == 2, -value, value)


def silu(value):
    half = 0.5 * value
    return half + half * jnp.tanh(half)


def dot(a, b):
    return jnp.dot(a, b, preferred_element_type=jnp.float32)


INPUTS = 16


def writer(feat_in, energy_in, forces_in, feat_out, energy_out, forces_out, sems):
    pairs = ((feat_in, feat_out), (energy_in, energy_out), (forces_in, forces_out))
    copies = [pltpu.make_async_copy(a, b, sems.at[i]) for i, (a, b) in enumerate(pairs)]
    for copy in copies:
        copy.start()
    for copy in copies:
        copy.wait()


def kernel(sizes, *refs):
    in_hbm, refs = refs[:INPUTS], refs[INPUTS:]
    (out_feat, out_energy, out_forces), refs = refs[:3], refs[3:]
    held, refs = refs[:INPUTS], refs[INPUTS:]
    (
        load_sem,
        ext,
        ph,
        fh,
        wgt,
        agg,
        own_rows,
        coords,
        q_all,
        qw,
        tb,
        gz_buf,
        mine,
        panel,
        part,
        part_buf,
        send_h,
        recv_h,
        send_c,
        recv_c,
        send_q,
        recv_q,
        send_g,
        recv_g,
        send_p,
        recv_p,
    ) = refs
    (
        species,
        sublayer,
        counts,
        offsets,
        feat,
        table,
        charge_w,
        cst,
        dist,
        near,
        centers,
        radial_in,
        radial_out,
        update_in,
        update_out,
        energy_w,
    ) = held
    loads = [
        pltpu.make_async_copy(a, b, load_sem.at[i]) for i, (a, b) in enumerate(zip(in_hbm, held))
    ]
    for load in loads:
        load.start()
    zc, xc, slots, entries, channels, n_xy, n_gz = sizes
    cells = zc * xc
    atoms = cells * slots
    layers = 2 * zc
    pairs = layers * channels
    f32, bf16, i32 = jnp.float32, jnp.bfloat16, jnp.int32
    exact = lax.Precision.HIGHEST
    iota = lax.broadcasted_iota
    width = feat.shape[1]
    gz = lax.axis_index("gz")
    xy = lax.axis_index("xy")
    left, right = lax.rem(xy + n_xy - 1, n_xy), lax.rem(xy + 1, n_xy)
    xy_peers = [lax.rem(xy + d, n_xy) for d in range(1, n_xy)]
    gz_peers = [lax.rem(gz + d, n_gz) for d in range(1, n_gz)]
    has_below = gz > 0
    has_above = gz < n_gz - 1

    barrier = pltpu.get_barrier_semaphore()
    for peer in xy_peers:
        pl.semaphore_signal(barrier, inc=1, device_id={"xy": peer}, device_id_type=MESH)
    for peer in gz_peers:
        pl.semaphore_signal(barrier, inc=1, device_id={"gz": peer}, device_id_type=MESH)
    for present, step in ((has_below, -1), (has_above, 1)):

        @pl.when(present)
        def _():
            for side in (left, right):
                pl.semaphore_signal(
                    barrier, inc=1, device_id={"gz": gz + step, "xy": side}, device_id_type=MESH
                )

    for load in loads[:4]:
        load.wait()
    unfold = (iota(i32, (slots, atoms), 1) % slots == iota(i32, (slots, atoms), 0)).astype(f32)
    own_cell = iota(i32, (cells, atoms), 1) // slots == iota(i32, (cells, atoms), 0)
    stacked = jnp.concatenate(
        [species[...].astype(f32), sublayer[...].astype(f32), counts[...].astype(f32), offsets[...]],
        axis=0,
    )
    wide = jnp.dot(stacked, unfold, precision=exact, preferred_element_type=f32)
    kind_row, sub_row, count_row, x_row, y_row = [
        jnp.sum(jnp.where(own_cell, wide[i * cells : (i + 1) * cells], 0.0), axis=0, keepdims=True)
        for i in range(5)
    ]
    atom_cell = iota(i32, (1, atoms), 1) // slots
    x_row = cell_width * (xy * xc + atom_cell % xc).astype(f32) + x_row
    layer_row = sub_row + (2 * (atom_cell // xc)).astype(f32)
    blank = jnp.zeros((3, atoms), f32)
    rows = jnp.concatenate([x_row, y_row, layer_row, kind_row, count_row, blank], axis=0)
    coords[xy] = rows
    cols = jnp.transpose(rows)

    for load in loads[4:7]:
        load.wait()
    kinds = table.shape[0]
    onehot = cols[:, 3:4] == iota(i32, (atoms, kinds), 1).astype(f32)
    hidden = (feat[...].astype(f32) + dot(onehot.astype(f32).astype(bf16), table[...])).astype(bf16)
    ext[1 : zc + 1, 1 : xc + 1] = hidden.reshape(zc, xc, slots, width)
    q_all[xy] = lax.dot_general(
        charge_w[...], hidden, (((1,), (1,)), ((), ())), preferred_element_type=f32
    ).astype(bf16)

    @pl.when(jnp.logical_not(has_below))
    def _():
        ext[0] = jnp.zeros(ext.shape[1:], bf16)

    @pl.when(jnp.logical_not(has_above))
    def _():
        ext[zc + 1] = jnp.zeros(ext.shape[1:], bf16)

    def strip_phases(strip):
        at = jnp.transpose(coords[strip])
        lane = iota(i32, (1, 128), 1)
        turn = jnp.where(lane % 64 < 32, 1, 0)
        first = lane < 64
        step = 64
        for start in range(0, atoms // 2, step):
            value = []
            for part in range(2):
                row = start + part * (atoms // 2)
                at_x, at_y = at[row : row + step, 0:1], at[row : row + step, 1:2]
                lines = pl.ds(strip * atoms + row, step)
                quadrant, sine, cosine = reduced(at_x * cst[xy, 0:1, :128] + at_y * cst[xy, 1:2, :128])
                ph[lines, :128] = at_quadrant(quadrant + 1, sine, cosine).astype(bf16)
                ph[lines, 128:256] = at_quadrant(quadrant, sine, cosine).astype(bf16)
                value.append(at_x * cst[xy, 0:1, 256:] + at_y * cst[xy, 1:2, 256:])
            quadrant, sine, cosine = reduced(jnp.where(first, value[0], value[1]))
            both = at_quadrant(quadrant + turn, sine, cosine)
            for part in range(2):
                lines = pl.ds(strip * atoms + start + part * (atoms // 2), step)
                ph[lines, 256:] = jnp.where(first == (part == 0), both, 0.0).astype(bf16)

    def strip_moments(strip):
        layer = coords[strip][2:3]
        charges = q_all[strip].astype(f32)
        weighted = jnp.concatenate(
            [jnp.where(layer == float(l), charges, 0.0) for l in range(layers)], axis=0
        ).astype(bf16)
        qw[strip] = weighted
        return dot(weighted, ph[pl.ds(strip * atoms, atoms), :])

    loads[7].wait()
    strip_phases(xy)
    total = strip_moments(xy)

    for load in loads[8:]:
        load.wait()
    d_all = dist[...]
    slot = iota(i32, (atoms, 1), 0) % slots
    entry = iota(i32, (atoms, entries), 1)
    usable = (entry < cols[:, 4:5].astype(i32)) & (near[...] != 4 * slots + slot)
    ratio = d_all * (1.0 / cutoff)
    envelope = 1.0 - ratio * ratio
    wgt[...] = jnp.where(usable, envelope * envelope, 0.0)
    basis_count, radial = radial_in.shape
    spread_shape = (entries, entries * basis_count)
    spread = (iota(i32, spread_shape, 1) // basis_count == iota(i32, spread_shape, 0)).astype(f32)
    d_high = d_all.astype(bf16)
    d_rest = d_all - d_high.astype(f32)
    d_mid = d_rest.astype(bf16)
    d_low = (d_rest - d_mid.astype(f32)).astype(bf16)
    spread = jnp.concatenate([spread] * 3, axis=0).astype(bf16)
    spacing = dot(jnp.concatenate([d_high, d_mid, d_low], axis=1), spread)
    gap = spacing - centers[0:1, :]
    basis = jnp.exp(-(gap * gap)).astype(bf16)

    diagonals = 2 * (has_below.astype(i32) + has_above.astype(i32))
    pl.semaphore_wait(barrier, n_xy - 1 + n_gz - 1 + diagonals)

    def remote(src, dst, send, recv, target):
        return pltpu.make_async_remote_copy(
            src_ref=src,
            dst_ref=dst,
            send_sem=send,
            recv_sem=recv,
            device_id=target,
            device_id_type=MESH,
        )

    strip_copies = []
    for d, peer in enumerate(xy_peers):
        strip_copies += [
            remote(coords.at[xy], coords.at[xy], send_c.at[d], recv_c.at[d], {"xy": peer}),
            remote(q_all.at[xy], q_all.at[xy], send_q.at[d], recv_q.at[d], {"xy": peer}),
        ]
    for copy in strip_copies:
        copy.start()

    inner = pl.ds(1, zc)
    x_copies = [
        remote(ext.at[inner, 1], ext.at[inner, xc + 1], send_h.at[0], recv_h.at[0], {"xy": left}),
        remote(ext.at[inner, xc], ext.at[inner, 0], send_h.at[1], recv_h.at[1], {"xy": right}),
    ]

    def z_copies(first, own, ghost, target):
        strip = pl.ds(1, xc)
        return [
            remote(ext.at[own, strip], ext.at[ghost, strip], send_h.at[first], recv_h.at[first], {"gz": target}),
            remote(ext.at[own, 1], ext.at[ghost, xc + 1], send_h.at[first + 1], recv_h.at[first + 1], {"gz": target, "xy": left}),
            remote(ext.at[own, xc], ext.at[ghost, 0], send_h.at[first + 2], recv_h.at[first + 2], {"gz": target, "xy": right}),
        ]

    down = z_copies(2, 1, zc + 1, gz - 1)
    rise = z_copies(5, zc, 0, gz + 1)
    for copy in x_copies:
        copy.start()

    @pl.when(has_below)
    def _():
        for copy in down:
            copy.start()

    @pl.when(has_above)
    def _():
        for copy in rise:
            copy.start()


    group = 128 // basis_count
    tall = jnp.concatenate([radial_in[...].astype(f32)] * group, axis=0)
    flat = jnp.concatenate([tall] * group, axis=1)
    diagonal = iota(i32, flat.shape, 0) // basis_count == iota(i32, flat.shape, 1) // radial
    hidden_in = jnp.where(diagonal, flat, 0.0).astype(bf16)
    for block in range(entries // group):
        for tile in range(flat.shape[1] // 256):
            pre = dot(basis[:, block * 128 : (block + 1) * 128], hidden_in[:, tile * 256 : (tile + 1) * 256])
            first = block * flat.shape[1] + tile * 256
            fh[:, first : first + 256] = silu(pre).astype(bf16)
    pack = 128 // radial
    tall = jnp.concatenate([radial_out[...].astype(f32)] * pack, axis=0)
    flat = jnp.concatenate([tall] * pack, axis=1)
    diagonal = iota(i32, flat.shape, 0) // radial == iota(i32, flat.shape, 1) // width
    hidden_out = jnp.where(diagonal, flat, 0.0).astype(bf16)

    for copy in strip_copies:
        copy.wait()

    def add_strip(d, total):
        strip = lax.rem(xy + d, n_xy)
        strip_phases(strip)
        return total + strip_moments(strip)

    total = lax.fori_loop(1, n_xy, add_strip, total, unroll=3)
    spare = total[:, 256:]
    mine[:, :256] = total[:, :256]
    mine[:, 256:] = spare + jnp.concatenate([spare[:, 64:], spare[:, :64]], axis=1)

    def power(n):
        return cst[xy, 5 + n : 6 + n, :]

    def layer_moments(l):
        return mine[l * channels : (l + 1) * channels, :]

    tb[0] = sum(layer_moments(l) * power(layers - 1 - l) for l in range(layers))
    tb[1] = sum(layer_moments(l) * power(l) for l in range(layers))
    gz_copies = [
        remote(tb.at[jnp.where(peer > gz, 0, 1)], gz_buf.at[gz], send_g.at[d], recv_g.at[d], {"gz": peer})
        for d, peer in enumerate(gz_peers)
    ]
    for copy in gz_copies:
        copy.start()

    for copy in x_copies:
        copy.wait()

    @pl.when(has_below)
    def _():
        for copy in down:
            copy.wait_send()
        for copy in rise:
            copy.wait_recv()

    @pl.when(has_above)
    def _():
        for copy in rise:
            copy.wait_send()
        for copy in down:
            copy.wait_recv()

    half = 9 * slots // 2
    codes = iota(i32, (slots, half), 1).astype(f32).astype(bf16)
    hit, miss = jnp.ones(codes.shape, bf16), jnp.zeros(codes.shape, bf16)

    def edge_row(z):
        def one(x, carry):
            base = pl.multiple_of((z * xc + x) * slots, slots)
            region = ext[z : z + 3, pl.ds(x, 3)].reshape(9 * slots, width)
            region = jnp.concatenate([region[:half], region[half:]], axis=1)
            index = near[pl.ds(base, slots), :]
            upper = index >= half
            folded = jnp.where(upper, index - half, index).astype(f32).astype(bf16)
            weight = wgt[pl.ds(base, slots), :]
            signed = jnp.where(upper, -weight, weight)
            chosen = jnp.concatenate(
                [jnp.where(folded[:, e : e + 1] == codes, hit, miss) for e in range(entries)], axis=0
            )
            gathered = dot(chosen, region)
            hid = fh[pl.ds(base, slots), :]
            both = jnp.concatenate(
                [hid[:, p * 128 : (p + 1) * 128] for p in range(hid.shape[1] // 128)], axis=0
            )
            filters = dot(both, hidden_out)
            acc = jnp.zeros((slots, width), f32)
            for e in range(entries):
                row, col = (e // pack) * slots, (e % pack) * width
                mark = jnp.broadcast_to(signed[:, e : e + 1], (slots, width))
                filtered = jnp.abs(mark) * filters[row : row + slots, col : col + width]
                pair = gathered[e * slots : (e + 1) * slots]
                rows_of = jnp.where(mark < 0.0, pair[:, width:], pair[:, :width])
                acc = acc + filtered * rows_of
            agg[pl.ds(base, slots), :] = acc.astype(bf16)
            return carry

        lax.fori_loop(0, xc, one, 0, unroll=4)

    for z in range(zc // 2):
        edge_row(z)

    for copy in gz_copies:
        copy.wait()
    span = power(layers)
    none = jnp.zeros(tb.shape[1:], f32)
    from_below = lax.fori_loop(0, gz, lambda t, s: s * span + gz_buf[t], none)
    from_above = lax.fori_loop(0, n_gz - 1 - gz, lambda t, s: s * span + gz_buf[n_gz - 1 - t], none)
    for l in range(layers):
        value = power(l + 1) * from_below + power(layers - l) * from_above
        for m in range(layers):
            value = value + power(abs(l - m)) * layer_moments(m)
        value = value * cst[xy, 2:3, :]
        swapped = jnp.concatenate(
            [value[:, 128:256], value[:, :128]]
            + [value[:, 256 + 32 * n : 288 + 32 * n] for n in (1, 0, 3, 2)],
            axis=1,
        )
        lines = (value, cst[xy, 3:4, :] * swapped, cst[xy, 4:5, :] * swapped)
        for r, line in enumerate(lines):
            top = r * pairs + l * channels
            panel[top : top + channels, :] = line.astype(bf16)

    def strip_sums(strip):
        evaluated = lax.dot_general(
            panel[...],
            ph[pl.ds(strip * atoms, atoms), :],
            (((1,), (1,)), ((), ())),
            preferred_element_type=f32,
        )
        charges = qw[strip].astype(f32)
        lines = [
            jnp.sum(evaluated[r * pairs : (r + 1) * pairs] * charges, axis=0, keepdims=True)
            for r in range(3)
        ]
        return jnp.concatenate(lines + [jnp.zeros((5, atoms), f32)], axis=0)

    part_copies = []
    for d, peer in enumerate(xy_peers):
        part[d] = strip_sums(peer)
        copy = remote(part.at[d], part_buf.at[d], send_p.at[d], recv_p.at[d], {"xy": peer})
        copy.start()
        part_copies.append(copy)
    own_rows[...] = strip_sums(xy)

    for z in range(zc // 2, zc):
        edge_row(z)

    updated = silu(dot(agg[...], update_in[...])).astype(bf16)
    renewed = ext[1 : zc + 1, 1 : xc + 1].reshape(atoms, width).astype(f32) + dot(updated, update_out[...])
    out_feat[...] = renewed.astype(bf16)
    readout = jnp.broadcast_to(energy_w[0:1, :].astype(f32), (8, width))
    energy = lax.dot_general(
        readout, renewed, (((1,), (1,)), ((), ())), precision=exact, preferred_element_type=f32
    )

    for copy in part_copies:
        copy.wait()
    sums = own_rows[...]
    for d in range(n_xy - 1):
        sums = sums + part_buf[d]
    finals = (energy[0:1] + 0.5 * sums[0:1], -sums[1:2], -sums[2:3])
    spread_out = jnp.concatenate([jnp.where(own_cell, line, 0.0) for line in finals], axis=0)
    folded = lax.dot_general(
        spread_out, unfold, (((1,), (1,)), ((), ())), precision=exact, preferred_element_type=f32
    )
    out_energy[...] = folded[:cells]
    out_forces[...] = folded[cells:]


def shards(
    n_xy,
    n_gz,
    features,
    species,
    sublayer,
    offsets,
    neighbours,
    neighbour_count,
    distances,
    species_table,
    charge_weight,
    radial_in,
    radial_out,
    update_in,
    update_out,
    energy_weight,
):
    f32, bf16 = jnp.float32, jnp.bfloat16
    zc, xc, slots, width = features.shape
    entries = neighbours.shape[3]
    channels = charge_weight.shape[1]
    cells = zc * xc
    atoms = cells * slots
    layers = 2 * zc
    pairs = layers * channels
    basis_count, radial = radial_in.shape
    cst = wave_constants(cell_width * (xc * n_xy), layers, n_xy)
    mids = np.float32(cutoff) * np.arange(basis_count).astype(np.float32) / np.float32(basis_count - 1)
    centers = np.tile(mids, (8, entries)).astype(np.float32)
    sizes = (zc, xc, slots, entries, channels, n_xy, n_gz)
    dma = pltpu.SemaphoreType.DMA
    vmem = pl.BlockSpec(memory_space=pltpu.VMEM)
    operands = (
        species.reshape(cells, slots),
        sublayer.reshape(cells, slots),
        neighbour_count.reshape(cells, slots),
        offsets.reshape(2 * cells, slots),
        features.reshape(atoms, width),
        species_table,
        charge_weight.T,
        jnp.asarray(cst),
        distances.reshape(atoms, entries),
        neighbours.reshape(atoms, entries),
        jnp.asarray(centers),
        radial_in,
        radial_out,
        update_in,
        update_out,
        energy_weight.reshape(1, width),
    )
    hbm = pl.BlockSpec(memory_space=pltpu.HBM)
    shapes = (
        jax.ShapeDtypeStruct((atoms, width), bf16),
        jax.ShapeDtypeStruct((cells, slots), f32),
        jax.ShapeDtypeStruct((2 * cells, slots), f32),
    )
    results = pl.pallas_call(
        functools.partial(kernel, sizes),
        out_shape=shapes,
        in_specs=[hbm] * INPUTS,
        out_specs=(vmem, vmem, vmem),
        scratch_shapes=[pltpu.VMEM(a.shape, a.dtype) for a in operands]
        + [
            dma((INPUTS,)),
            pltpu.VMEM((zc + 2, xc + 2, slots, width), bf16),
            pltpu.VMEM((n_xy * atoms, LANES), bf16),
            pltpu.VMEM((atoms, entries * radial), bf16),
            pltpu.VMEM((atoms, entries), f32),
            pltpu.VMEM((atoms, width), bf16),
            pltpu.VMEM((8, atoms), f32),
            pltpu.VMEM((n_xy, 8, atoms), f32),
            pltpu.VMEM((n_xy, channels, atoms), bf16),
            pltpu.VMEM((n_xy, pairs, atoms), bf16),
            pltpu.VMEM((2, channels, LANES), f32),
            pltpu.VMEM((n_gz, channels, LANES), f32),
            pltpu.VMEM((pairs, LANES), f32),
            pltpu.VMEM((3 * pairs, LANES), bf16),
            pltpu.VMEM((n_xy - 1, 8, atoms), f32),
            pltpu.VMEM((n_xy - 1, 8, atoms), f32),
            dma((8,)),
            dma((8,)),
            dma((n_xy - 1,)),
            dma((n_xy - 1,)),
            dma((n_xy - 1,)),
            dma((n_xy - 1,)),
            dma((n_gz - 1,)),
            dma((n_gz - 1,)),
            dma((n_xy - 1,)),
            dma((n_xy - 1,)),
        ],
        compiler_params=pltpu.CompilerParams(
            collective_id=0, has_side_effects=True, vmem_limit_bytes=60 * 1024 * 1024
        ),
        cost_estimate=pl.CostEstimate(flops=2_000_000_000, bytes_accessed=2_000_000, transcendentals=2_000_000),
    )(*operands)
    out_feat, energy, forces = pl.pallas_call(
        writer,
        out_shape=shapes,
        in_specs=[vmem] * 3,
        out_specs=(hbm, hbm, hbm),
        scratch_shapes=[dma((3,))],
    )(*results)
    return (
        out_feat.reshape(features.shape),
        energy.reshape(species.shape),
        forces.reshape((2,) + species.shape),
    )


def solution(mesh):
    atom = P(("groups", "gz"), "xy", None)
    atom_wide = P(("groups", "gz"), "xy", None, None)
    pair = P(None, ("groups", "gz"), "xy", None)
    in_specs = (atom_wide, atom, atom, pair, atom_wide, atom, atom_wide) + (P(),) * 7
    body = functools.partial(shards, mesh.shape["xy"], mesh.shape["gz"])
    return jax.shard_map(
        body, mesh=mesh, in_specs=in_specs, out_specs=(atom_wide, atom, pair), check_vma=False
    )
```

```python
import functools
import math

import jax
import jax.numpy as jnp
import numpy as np
from jax import lax
from jax.experimental import pallas as pl
from jax.experimental.pallas import tpu as pltpu
from jax.sharding import PartitionSpec as P

KX = 128
KY = 8
MESH = pl.DeviceIdType.MESH

cell_width = 11.0
layer_depth = 5.5
screening = 0.025
smearing = 1.0
coupling = 0.25
cutoff = 8.0

BLOCKS = (4, 0, 5, 6, 7)
LANES = 384


def wave_constants(width_x, layers, n_xy):
    f32 = np.float32
    per = KX // n_xy

    def factors(index_x, index_y, count):
        wave_x = f32(2.0 * math.pi / width_x) * (index_x - KX // 2).astype(f32)
        wave_y = f32(2.0 * math.pi / cell_width) * (index_y - KY // 2).astype(f32)
        square = wave_x * wave_x + wave_y * wave_y
        screened = np.sqrt(square + f32(screening * screening))
        weight = f32(coupling * (2.0 * math.pi / (width_x * cell_width))) * np.exp(
            f32(-0.5 * smearing * smearing) * square
        )
        quarter_x = (4.0 / width_x * (index_x - KX // 2)).astype(f32)
        quarter_y = (4.0 / cell_width * (index_y - KY // 2)).astype(f32)
        return wave_x, wave_y, weight / screened * count, screened, quarter_x, quarter_y

    strips = []
    for strip in range(n_xy):
        own = np.arange(strip * per, (strip + 1) * per)
        index_x = np.tile(own, len(BLOCKS) - 1)
        index_y = np.repeat(np.array(BLOCKS[1:]), per)
        count = np.where((index_y > KY // 2) & (index_x > 0), 2.0, 1.0).astype(f32)
        part_a = factors(index_x, index_y, count)
        index_x, index_y = own.copy(), np.full(per, KY // 2)
        count = np.where((own > 0) & (own < KX // 2), 2.0, 1.0).astype(f32)
        count[own > KX // 2] = 0.0
        for spare, j in enumerate((1, 2, 3)):
            place = KX // 2 + 1 + spare
            count[own == place] = 1.0
            index_y[own == place] = j
            index_x[own == place] = 0
        part_b = factors(index_x, index_y, count)
        lanes = []
        for one, two in zip(part_a, part_b):
            one = np.pad(one, (0, 128 - one.size))
            two = np.pad(two, (0, 32 - two.size))
            lanes.append(np.concatenate([one, one, two, two, np.zeros(64)]).astype(f32))
        wave_x, wave_y, weight, screened, *quarters = lanes
        sign = np.repeat(np.array([1, -1, 1, -1, 0], f32), [128, 128, 32, 32, 64])
        powers = [np.exp(-screened * f32(layer_depth) * f32(n)) for n in range(layers + 1)]
        rows = [*quarters, weight, sign * wave_x, sign * wave_y] + powers
        rows += [np.zeros(LANES, f32)] * (-len(rows) % 8)
        strips.append(np.stack(rows))
    return np.stack(strips).astype(f32)


def reduced(quarters):
    whole = (quarters + 12582912.0) - 12582912.0
    rest = quarters - whole
    square = rest * rest
    q = math.pi / 2.0
    sine = rest * (
        (((-1.9515295891e-4 * q**7) * square + 8.3321608736e-3 * q**5) * square - 1.6666654611e-1 * q**3)
        * square
        + q
    )
    cosine = (
        (((2.443315711809948e-5 * q**8) * square - 1.388731625493765e-3 * q**6) * square
         + 4.166664568298827e-2 * q**4) * square - 0.5 * q**2
    ) * square + 1.0
    return whole.astype(jnp.int32), sine, cosine


def at_quadrant(quadrant, sine, cosine):
    value = jnp.where((quadrant & 1) == 1, cosine, sine)
    return jnp.where((quadrant & 2) == 2, -value, value)


def silu(value):
    half = 0.5 * value
    return half + half * jnp.tanh(half)


def dot(a, b):
    return jnp.dot(a, b, preferred_element_type=jnp.float32)


INPUTS = 16


def writer(feat_in, energy_in, forces_in, feat_out, energy_out, forces_out, sems):
    pairs = ((feat_in, feat_out), (energy_in, energy_out), (forces_in, forces_out))
    copies = [pltpu.make_async_copy(a, b, sems.at[i]) for i, (a, b) in enumerate(pairs)]
    for copy in copies:
        copy.start()
    for copy in copies:
        copy.wait()


def kernel(sizes, *refs):
    in_hbm, refs = refs[:INPUTS], refs[INPUTS:]
    (out_feat, out_energy, out_forces), refs = refs[:3], refs[3:]
    held, refs = refs[:INPUTS], refs[INPUTS:]
    (
        load_sem,
        ext,
        ph,
        fh,
        wgt,
        agg,
        own_rows,
        coords,
        q_all,
        qw,
        tb,
        gz_buf,
        mine,
        panel,
        part,
        part_buf,
        send_h,
        recv_h,
        send_c,
        recv_c,
        send_q,
        recv_q,
        send_g,
        recv_g,
        send_p,
        recv_p,
    ) = refs
    (
        species,
        sublayer,
        counts,
        offsets,
        feat,
        table,
        charge_w,
        cst,
        dist,
        near,
        centers,
        radial_in,
        radial_out,
        update_in,
        update_out,
        energy_w,
    ) = held
    loads = [
        pltpu.make_async_copy(a, b, load_sem.at[i]) for i, (a, b) in enumerate(zip(in_hbm, held))
    ]
    for load in loads:
        load.start()
    zc, xc, slots, entries, channels, n_xy, n_gz = sizes
    cells = zc * xc
    atoms = cells * slots
    layers = 2 * zc
    pairs = layers * channels
    f32, bf16, i32 = jnp.float32, jnp.bfloat16, jnp.int32
    exact = lax.Precision.HIGHEST
    iota = lax.broadcasted_iota
    width = feat.shape[1]
    gz = lax.axis_index("gz")
    xy = lax.axis_index("xy")
    left, right = lax.rem(xy + n_xy - 1, n_xy), lax.rem(xy + 1, n_xy)
    xy_peers = [lax.rem(xy + d, n_xy) for d in range(1, n_xy)]
    gz_peers = [lax.rem(gz + d, n_gz) for d in range(1, n_gz)]
    has_below = gz > 0
    has_above = gz < n_gz - 1

    barrier = pltpu.get_barrier_semaphore()
    for peer in xy_peers:
        pl.semaphore_signal(barrier, inc=1, device_id={"xy": peer}, device_id_type=MESH)
    for peer in gz_peers:
        pl.semaphore_signal(barrier, inc=1, device_id={"gz": peer}, device_id_type=MESH)
    for present, step in ((has_below, -1), (has_above, 1)):

        @pl.when(present)
        def _():
            for side in (left, right):
                pl.semaphore_signal(
                    barrier, inc=1, device_id={"gz": gz + step, "xy": side}, device_id_type=MESH
                )

    for load in loads[:4]:
        load.wait()
    unfold = (iota(i32, (slots, atoms), 1) % slots == iota(i32, (slots, atoms), 0)).astype(f32)
    own_cell = iota(i32, (cells, atoms), 1) // slots == iota(i32, (cells, atoms), 0)
    stacked = jnp.concatenate(
        [species[...].astype(f32), sublayer[...].astype(f32), counts[...].astype(f32), offsets[...]],
        axis=0,
    )
    wide = jnp.dot(stacked, unfold, precision=exact, preferred_element_type=f32)
    kind_row, sub_row, count_row, x_row, y_row = [
        jnp.sum(jnp.where(own_cell, wide[i * cells : (i + 1) * cells], 0.0), axis=0, keepdims=True)
        for i in range(5)
    ]
    atom_cell = iota(i32, (1, atoms), 1) // slots
    x_row = cell_width * (xy * xc + atom_cell % xc).astype(f32) + x_row
    layer_row = sub_row + (2 * (atom_cell // xc)).astype(f32)
    blank = jnp.zeros((3, atoms), f32)
    rows = jnp.concatenate([x_row, y_row, layer_row, kind_row, count_row, blank], axis=0)
    coords[xy] = rows
    cols = jnp.transpose(rows)

    for load in loads[4:7]:
        load.wait()
    kinds = table.shape[0]
    onehot = cols[:, 3:4] == iota(i32, (atoms, kinds), 1).astype(f32)
    hidden = (feat[...].astype(f32) + dot(onehot.astype(f32).astype(bf16), table[...])).astype(bf16)
    ext[1 : zc + 1, 1 : xc + 1] = hidden.reshape(zc, xc, slots, width)
    q_all[xy] = lax.dot_general(
        charge_w[...], hidden, (((1,), (1,)), ((), ())), preferred_element_type=f32
    ).astype(bf16)

    @pl.when(jnp.logical_not(has_below))
    def _():
        ext[0] = jnp.zeros(ext.shape[1:], bf16)

    @pl.when(jnp.logical_not(has_above))
    def _():
        ext[zc + 1] = jnp.zeros(ext.shape[1:], bf16)

    def strip_phases(strip):
        at_x, at_y = coords[strip][0:1], coords[strip][1:2]
        step = 32
        for start in range(0, 128, step):
            here = slice(start, start + step)
            quadrant, sine, cosine = reduced(waves[here, 0:1] * at_x + waves[here, 1:2] * at_y)
            ph[strip, start : start + step] = at_quadrant(quadrant + 1, sine, cosine).astype(bf16)
            ph[strip, 128 + start : 128 + start + step] = at_quadrant(quadrant, sine, cosine).astype(bf16)
        quadrant, sine, cosine = reduced(waves[256:288, 0:1] * at_x + waves[256:288, 1:2] * at_y)
        ph[strip, 256:288] = at_quadrant(quadrant + 1, sine, cosine).astype(bf16)
        ph[strip, 288:320] = at_quadrant(quadrant, sine, cosine).astype(bf16)
        ph[strip, 320:] = jnp.zeros((LANES - 320, atoms), bf16)

    def strip_moments(strip):
        layer = coords[strip][2:3]
        charges = q_all[strip].astype(f32)
        weighted = jnp.concatenate(
            [jnp.where(layer == float(l), charges, 0.0) for l in range(layers)], axis=0
        ).astype(bf16)
        qw[strip] = weighted
        return lax.dot_general(
            ph[strip], weighted, (((1,), (1,)), ((), ())), preferred_element_type=f32
        )

    loads[7].wait()
    waves = jnp.transpose(cst[xy, 0:8, :])
    strip_phases(xy)
    total = strip_moments(xy)

    for load in loads[8:]:
        load.wait()
    d_all = dist[...]
    slot = iota(i32, (atoms, 1), 0) % slots
    entry = iota(i32, (atoms, entries), 1)
    usable = (entry < cols[:, 4:5].astype(i32)) & (near[...] != 4 * slots + slot)
    ratio = d_all * (1.0 / cutoff)
    envelope = 1.0 - ratio * ratio
    wgt[...] = jnp.where(usable, envelope * envelope, 0.0)
    basis_count, radial = radial_in.shape
    spread_shape = (entries, entries * basis_count)
    spread = (iota(i32, spread_shape, 1) // basis_count == iota(i32, spread_shape, 0)).astype(f32)
    d_high = d_all.astype(bf16)
    d_rest = d_all - d_high.astype(f32)
    d_mid = d_rest.astype(bf16)
    d_low = (d_rest - d_mid.astype(f32)).astype(bf16)
    spread = jnp.concatenate([spread] * 3, axis=0).astype(bf16)
    spacing = dot(jnp.concatenate([d_high, d_mid, d_low], axis=1), spread)
    gap = spacing - centers[0:1, :]
    basis = jnp.exp(-(gap * gap)).astype(bf16)

    diagonals = 2 * (has_below.astype(i32) + has_above.astype(i32))
    pl.semaphore_wait(barrier, n_xy - 1 + n_gz - 1 + diagonals)

    def remote(src, dst, send, recv, target):
        return pltpu.make_async_remote_copy(
            src_ref=src,
            dst_ref=dst,
            send_sem=send,
            recv_sem=recv,
            device_id=target,
            device_id_type=MESH,
        )

    strip_copies = []
    for d, peer in enumerate(xy_peers):
        strip_copies += [
            remote(coords.at[xy], coords.at[xy], send_c.at[d], recv_c.at[d], {"xy": peer}),
            remote(q_all.at[xy], q_all.at[xy], send_q.at[d], recv_q.at[d], {"xy": peer}),
        ]
    for copy in strip_copies:
        copy.start()

    inner = pl.ds(1, zc)
    x_copies = [
        remote(ext.at[inner, 1], ext.at[inner, xc + 1], send_h.at[0], recv_h.at[0], {"xy": left}),
        remote(ext.at[inner, xc], ext.at[inner, 0], send_h.at[1], recv_h.at[1], {"xy": right}),
    ]

    def z_copies(first, own, ghost, target):
        strip = pl.ds(1, xc)
        return [
            remote(ext.at[own, strip], ext.at[ghost, strip], send_h.at[first], recv_h.at[first], {"gz": target}),
            remote(ext.at[own, 1], ext.at[ghost, xc + 1], send_h.at[first + 1], recv_h.at[first + 1], {"gz": target, "xy": left}),
            remote(ext.at[own, xc], ext.at[ghost, 0], send_h.at[first + 2], recv_h.at[first + 2], {"gz": target, "xy": right}),
        ]

    down = z_copies(2, 1, zc + 1, gz - 1)
    rise = z_copies(5, zc, 0, gz + 1)
    for copy in x_copies:
        copy.start()

    @pl.when(has_below)
    def _():
        for copy in down:
            copy.start()

    @pl.when(has_above)
    def _():
        for copy in rise:
            copy.start()


    group = 128 // basis_count
    tall = jnp.concatenate([radial_in[...].astype(f32)] * group, axis=0)
    flat = jnp.concatenate([tall] * group, axis=1)
    diagonal = iota(i32, flat.shape, 0) // basis_count == iota(i32, flat.shape, 1) // radial
    hidden_in = jnp.where(diagonal, flat, 0.0).astype(bf16)
    for block in range(entries // group):
        for tile in range(flat.shape[1] // 256):
            pre = dot(basis[:, block * 128 : (block + 1) * 128], hidden_in[:, tile * 256 : (tile + 1) * 256])
            first = block * flat.shape[1] + tile * 256
            fh[:, first : first + 256] = silu(pre).astype(bf16)
    pack = 128 // radial
    tall = jnp.concatenate([radial_out[...].astype(f32)] * pack, axis=0)
    flat = jnp.concatenate([tall] * pack, axis=1)
    diagonal = iota(i32, flat.shape, 0) // radial == iota(i32, flat.shape, 1) // width
    hidden_out = jnp.where(diagonal, flat, 0.0).astype(bf16)

    for copy in strip_copies:
        copy.wait()

    def add_strip(d, total):
        strip = lax.rem(xy + d, n_xy)
        strip_phases(strip)
        return total + strip_moments(strip)

    total = lax.fori_loop(1, n_xy, add_strip, total, unroll=3)
    mine[...] = jnp.transpose(total)

    def power(n):
        return cst[xy, 5 + n : 6 + n, :]

    def layer_moments(l):
        return mine[l * channels : (l + 1) * channels, :]

    tb[0] = sum(layer_moments(l) * power(layers - 1 - l) for l in range(layers))
    tb[1] = sum(layer_moments(l) * power(l) for l in range(layers))
    gz_copies = [
        remote(tb.at[jnp.where(peer > gz, 0, 1)], gz_buf.at[gz], send_g.at[d], recv_g.at[d], {"gz": peer})
        for d, peer in enumerate(gz_peers)
    ]
    for copy in gz_copies:
        copy.start()

    for copy in x_copies:
        copy.wait()

    @pl.when(has_below)
    def _():
        for copy in down:
            copy.wait_send()
        for copy in rise:
            copy.wait_recv()

    @pl.when(has_above)
    def _():
        for copy in rise:
            copy.wait_send()
        for copy in down:
            copy.wait_recv()

    half = 9 * slots // 2
    codes = iota(i32, (slots, half), 1).astype(f32).astype(bf16)
    hit, miss = jnp.ones(codes.shape, bf16), jnp.zeros(codes.shape, bf16)

    def edge_row(z):
        def one(x, carry):
            base = pl.multiple_of((z * xc + x) * slots, slots)
            region = ext[z : z + 3, pl.ds(x, 3)].reshape(9 * slots, width)
            region = jnp.concatenate([region[:half], region[half:]], axis=1)
            index = near[pl.ds(base, slots), :]
            upper = index >= half
            folded = jnp.where(upper, index - half, index).astype(f32).astype(bf16)
            weight = wgt[pl.ds(base, slots), :]
            signed = jnp.where(upper, -weight, weight)
            chosen = jnp.concatenate(
                [jnp.where(folded[:, e : e + 1] == codes, hit, miss) for e in range(entries)], axis=0
            )
            gathered = dot(chosen, region)
            hid = fh[pl.ds(base, slots), :]
            both = jnp.concatenate(
                [hid[:, p * 128 : (p + 1) * 128] for p in range(hid.shape[1] // 128)], axis=0
            )
            filters = dot(both, hidden_out)
            acc = jnp.zeros((slots, width), f32)
            for e in range(entries):
                row, col = (e // pack) * slots, (e % pack) * width
                mark = jnp.broadcast_to(signed[:, e : e + 1], (slots, width))
                filtered = jnp.abs(mark) * filters[row : row + slots, col : col + width]
                pair = gathered[e * slots : (e + 1) * slots]
                rows_of = jnp.where(mark < 0.0, pair[:, width:], pair[:, :width])
                acc = acc + filtered * rows_of
            agg[pl.ds(base, slots), :] = acc.astype(bf16)
            return carry

        lax.fori_loop(0, xc, one, 0, unroll=4)

    for z in range(zc // 2):
        edge_row(z)

    for copy in gz_copies:
        copy.wait()
    span = power(layers)
    none = jnp.zeros(tb.shape[1:], f32)
    from_below = lax.fori_loop(0, gz, lambda t, s: s * span + gz_buf[t], none)
    from_above = lax.fori_loop(0, n_gz - 1 - gz, lambda t, s: s * span + gz_buf[n_gz - 1 - t], none)
    for l in range(layers):
        value = power(l + 1) * from_below + power(layers - l) * from_above
        for m in range(layers):
            value = value + power(abs(l - m)) * layer_moments(m)
        value = value * cst[xy, 2:3, :]
        swapped = jnp.concatenate(
            [value[:, 128:256], value[:, :128]]
            + [value[:, 288:320], value[:, 256:288], value[:, 320:]],
            axis=1,
        )
        lines = (value, cst[xy, 3:4, :] * swapped, cst[xy, 4:5, :] * swapped)
        for r, line in enumerate(lines):
            top = r * pairs + l * channels
            panel[top : top + channels, :] = line.astype(bf16)

    def strip_sums(strip):
        evaluated = dot(panel[...], ph[strip])
        charges = qw[strip].astype(f32)
        lines = [
            jnp.sum(evaluated[r * pairs : (r + 1) * pairs] * charges, axis=0, keepdims=True)
            for r in range(3)
        ]
        return jnp.concatenate(lines + [jnp.zeros((5, atoms), f32)], axis=0)

    part_copies = []
    for d, peer in enumerate(xy_peers):
        part[d] = strip_sums(peer)
        copy = remote(part.at[d], part_buf.at[d], send_p.at[d], recv_p.at[d], {"xy": peer})
        copy.start()
        part_copies.append(copy)
    own_rows[...] = strip_sums(xy)

    for z in range(zc // 2, zc):
        edge_row(z)

    updated = silu(dot(agg[...], update_in[...])).astype(bf16)
    renewed = ext[1 : zc + 1, 1 : xc + 1].reshape(atoms, width).astype(f32) + dot(updated, update_out[...])
    out_feat[...] = renewed.astype(bf16)
    readout = jnp.broadcast_to(energy_w[0:1, :].astype(f32), (8, width))
    energy = lax.dot_general(
        readout, renewed, (((1,), (1,)), ((), ())), precision=exact, preferred_element_type=f32
    )

    for copy in part_copies:
        copy.wait()
    sums = own_rows[...]
    for d in range(n_xy - 1):
        sums = sums + part_buf[d]
    finals = (energy[0:1] + 0.5 * sums[0:1], -sums[1:2], -sums[2:3])
    spread_out = jnp.concatenate([jnp.where(own_cell, line, 0.0) for line in finals], axis=0)
    folded = lax.dot_general(
        spread_out, unfold, (((1,), (1,)), ((), ())), precision=exact, preferred_element_type=f32
    )
    out_energy[...] = folded[:cells]
    out_forces[...] = folded[cells:]


def shards(
    n_xy,
    n_gz,
    features,
    species,
    sublayer,
    offsets,
    neighbours,
    neighbour_count,
    distances,
    species_table,
    charge_weight,
    radial_in,
    radial_out,
    update_in,
    update_out,
    energy_weight,
):
    f32, bf16 = jnp.float32, jnp.bfloat16
    zc, xc, slots, width = features.shape
    entries = neighbours.shape[3]
    channels = charge_weight.shape[1]
    cells = zc * xc
    atoms = cells * slots
    layers = 2 * zc
    pairs = layers * channels
    basis_count, radial = radial_in.shape
    cst = wave_constants(cell_width * (xc * n_xy), layers, n_xy)
    mids = np.float32(cutoff) * np.arange(basis_count).astype(np.float32) / np.float32(basis_count - 1)
    centers = np.tile(mids, (8, entries)).astype(np.float32)
    sizes = (zc, xc, slots, entries, channels, n_xy, n_gz)
    dma = pltpu.SemaphoreType.DMA
    vmem = pl.BlockSpec(memory_space=pltpu.VMEM)
    operands = (
        species.reshape(cells, slots),
        sublayer.reshape(cells, slots),
        neighbour_count.reshape(cells, slots),
        offsets.reshape(2 * cells, slots),
        features.reshape(atoms, width),
        species_table,
        charge_weight.T,
        jnp.asarray(cst),
        distances.reshape(atoms, entries),
        neighbours.reshape(atoms, entries),
        jnp.asarray(centers),
        radial_in,
        radial_out,
        update_in,
        update_out,
        energy_weight.reshape(1, width),
    )
    hbm = pl.BlockSpec(memory_space=pltpu.HBM)
    shapes = (
        jax.ShapeDtypeStruct((atoms, width), bf16),
        jax.ShapeDtypeStruct((cells, slots), f32),
        jax.ShapeDtypeStruct((2 * cells, slots), f32),
    )
    results = pl.pallas_call(
        functools.partial(kernel, sizes),
        out_shape=shapes,
        in_specs=[hbm] * INPUTS,
        out_specs=(vmem, vmem, vmem),
        scratch_shapes=[pltpu.VMEM(a.shape, a.dtype) for a in operands]
        + [
            dma((INPUTS,)),
            pltpu.VMEM((zc + 2, xc + 2, slots, width), bf16),
            pltpu.VMEM((n_xy, LANES, atoms), bf16),
            pltpu.VMEM((atoms, entries * radial), bf16),
            pltpu.VMEM((atoms, entries), f32),
            pltpu.VMEM((atoms, width), bf16),
            pltpu.VMEM((8, atoms), f32),
            pltpu.VMEM((n_xy, 8, atoms), f32),
            pltpu.VMEM((n_xy, channels, atoms), bf16),
            pltpu.VMEM((n_xy, pairs, atoms), bf16),
            pltpu.VMEM((2, channels, LANES), f32),
            pltpu.VMEM((n_gz, channels, LANES), f32),
            pltpu.VMEM((pairs, LANES), f32),
            pltpu.VMEM((3 * pairs, LANES), bf16),
            pltpu.VMEM((n_xy - 1, 8, atoms), f32),
            pltpu.VMEM((n_xy - 1, 8, atoms), f32),
            dma((8,)),
            dma((8,)),
            dma((n_xy - 1,)),
            dma((n_xy - 1,)),
            dma((n_xy - 1,)),
            dma((n_xy - 1,)),
            dma((n_gz - 1,)),
            dma((n_gz - 1,)),
            dma((n_xy - 1,)),
            dma((n_xy - 1,)),
        ],
        compiler_params=pltpu.CompilerParams(
            collective_id=0, has_side_effects=True, vmem_limit_bytes=60 * 1024 * 1024
        ),
        cost_estimate=pl.CostEstimate(flops=2_000_000_000, bytes_accessed=2_000_000, transcendentals=2_000_000),
    )(*operands)
    out_feat, energy, forces = pl.pallas_call(
        writer,
        out_shape=shapes,
        in_specs=[vmem] * 3,
        out_specs=(hbm, hbm, hbm),
        scratch_shapes=[dma((3,))],
    )(*results)
    return (
        out_feat.reshape(features.shape),
        energy.reshape(species.shape),
        forces.reshape((2,) + species.shape),
    )


def solution(mesh):
    atom = P(("groups", "gz"), "xy", None)
    atom_wide = P(("groups", "gz"), "xy", None, None)
    pair = P(None, ("groups", "gz"), "xy", None)
    in_specs = (atom_wide, atom, atom, pair, atom_wide, atom, atom_wide) + (P(),) * 7
    body = functools.partial(shards, mesh.shape["xy"], mesh.shape["gz"])
    return jax.shard_map(
        body, mesh=mesh, in_specs=in_specs, out_specs=(atom_wide, atom, pair), check_vma=False
    )
```
